256 devices in a mesh: leaf: 256 (over y, x, z, core).
Axes of the slice: x: 4, y: 4, z: 8, core: 2. Of those that a mesh axis runs over, the one named last changes fastest.
Arguments:
- features: float32 [8, 1048576], P(None, 'leaf'), as said below
- solution: float32 [64, 1048576], P(None, 'leaf'), may hold values from -6 to 6
- residual: float32 [64, 1048576], P(None, 'leaf')
- direction: float32 [64, 1048576], P(None, 'leaf')
- neighbours: int32 [4096, 8], P('leaf'), may hold values from -1 to 4095, as said below
- skeleton_basis: float32 [128, 1048576], P(None, 'leaf'), may hold values from -0.09375 to 0.09375
- base_skeleton: int32 [256, 128], P('leaf'), may hold values from 0 to 4095, as said below
- upper_skeleton: int32 [256, 8, 128], P('leaf'), may hold values from 0 to 255, as said below
- transfer: float32 [256, 8, 256, 128], P('leaf'), as said below
Outputs:
- new_solution: float32 [64, 1048576], P(None, 'leaf')
- new_residual: float32 [64, 1048576], P(None, 'leaf')
- new_direction: float32 [64, 1048576], P(None, 'leaf')
The draws below stay inside these ranges and needn't reach their ends.
Inputs may be any that keep to these rules, and one draw needn't show every extreme that they name: `neighbours`: row k lists the near-field partner leaves of leaf k by global leaf number, -1 for an empty slot; leaf j appears in row k exactly as often as k in row j, and no leaf lists itself. Slots 0 to 5 name leaves of the same device; on each device these slots are filled for a leading run of slots that is the same for all its leaves. Slot 6 names a leaf of the device before, slot 7 a leaf of the device after. On every device but the first exactly 4 leaves fill slot 6, and on every device but the last exactly 4 fill slot 7. No device has more than 104 filled slots, and some device has exactly that many. `base_skeleton`: each row holds 128 distinct point numbers within its device-level node. `upper_skeleton`: entry [n, l - 1] holds 128 distinct positions among the 256 skeleton points of the two children of the level-l node above node n; all nodes under one level-l node hold the same entry. `transfer`: all nodes under one level-l node hold the same matrix at [n, l - 1]. `features`: point coordinates, in tree order.
All inputs are finite; a program needn't handle non-finite values.
Results may differ from the reference program's by a relative error of at most 0.00055.
The reference program's roundings to bfloat16 on the way count: a program that leaves them out, or rounds other values in their place, can miss the bound.
Values may be sent and summed in bfloat16 or wider, within the bound.
A program may use at most 64 MiB of HBM per device.

```python
import math
import jax
import jax.numpy as jnp
from jax import lax

DIM = 8
NRHS = 64
SKEL = 128
LEAF = 256
SLOTS = 8
LEAVES_DEV = 16
BOUND = 4
LEVELS = 8
LEAVES = 4096
POINTS = 1048576
N_LEAF = 256


def draw_features(key, part):
    key = jax.random.fold_in(key, 1)
    key_freq, key_phase, key_noise = jax.random.split(key, 3)
    frequency = jax.random.uniform(key_freq, (DIM, 1), minval=1.0, maxval=6.0)
    phases = jax.random.uniform(key_phase, (DIM, 1), minval=-math.pi, maxval=math.pi)
    leaf_place = (jnp.arange(POINTS) // LEAF).astype(jnp.float32) / LEAVES
    centres = 1.5 * jnp.sin(2.0 * math.pi * frequency * leaf_place[None, :] + phases)
    jitter = 1.5 * jax.random.normal(key_noise, (DIM, POINTS))
    return (centres + jitter).astype(jnp.float32)


def class_field(key, trend_power):
    key_rows = jax.random.fold_in(key, 0)
    key_cols = jax.random.fold_in(key, 1)
    key_normal = jax.random.fold_in(key, 3)
    place = jnp.arange(POINTS).astype(jnp.float32) / POINTS
    trend = (0.5 + place) ** trend_power
    row_scale = jnp.exp(jax.random.uniform(key_rows, (1, POINTS), minval=math.log(0.3), maxval=math.log(3.0)))
    col_scale = jnp.exp(jax.random.uniform(key_cols, (NRHS, 1), minval=math.log(0.3), maxval=math.log(3.0)))
    own_normal = jax.random.normal(key_normal, (NRHS, POINTS))
    own_part = own_normal
    mixed = own_part
    return (trend[None, :] * row_scale * col_scale * mixed).astype(jnp.float32)


def draw_residual(key, part):
    key = jax.random.fold_in(key, 2)
    return class_field(key, 1.0)


def draw_direction(key, part):
    key = jax.random.fold_in(key, 3)
    return class_field(key, 1.0)


def draw_neighbours(key, part):
    key = jax.random.fold_in(key, 4)
    key_active, key_forced, key_inner, key_edge = jax.random.split(key, 4)
    inner_slots = SLOTS - 2
    device_no = jnp.arange(N_LEAF, dtype=jnp.int32)
    active = jax.random.randint(key_active, (N_LEAF,), 1, inner_slots + 1)
    forced = jax.random.randint(key_forced, (), 1, N_LEAF - 1)
    active = jnp.where(device_no == forced, inner_slots, active)

    def matching(match_key):
        shuffled = jax.random.permutation(match_key, LEAVES_DEV).astype(jnp.int32)
        places = jnp.argsort(shuffled).astype(jnp.int32)
        return shuffled[places ^ 1]

    def device_matchings(device_key):
        return jax.vmap(matching)(jax.random.split(device_key, inner_slots))
    partners = jax.vmap(device_matchings)(jax.random.split(key_inner, N_LEAF))
    offsets = (device_no * LEAVES_DEV)[:, None, None]
    in_use = jnp.arange(inner_slots)[None, :, None] < active[:, None, None]
    inner_ids = jnp.where(in_use, partners + offsets, -1)

    def edge_orders(edge_key):
        key_low, key_high = jax.random.split(edge_key)
        low_order = jax.random.permutation(key_low, LEAVES_DEV).astype(jnp.int32)
        high_order = jax.random.permutation(key_high, LEAVES_DEV).astype(jnp.int32)
        return (low_order, high_order, jnp.argsort(low_order).astype(jnp.int32), jnp.argsort(high_order).astype(jnp.int32))
    low_order, high_order, low_place, high_place = jax.vmap(edge_orders)(jax.random.split(key_edge, N_LEAF))
    column = device_no[:, None]
    right_partner = jnp.take_along_axis(high_order, low_place, axis=1)
    right_ids = jnp.where((low_place < BOUND) & (column < N_LEAF - 1), (column + 1) * LEAVES_DEV + right_partner, -1)
    prev_low = jnp.roll(low_order, 1, axis=0)
    prev_place = jnp.roll(high_place, 1, axis=0)
    left_partner = jnp.take_along_axis(prev_low, prev_place, axis=1)
    left_ids = jnp.where((prev_place < BOUND) & (column > 0), (column - 1) * LEAVES_DEV + left_partner, -1)
    slot_table = jnp.concatenate([inner_ids.transpose(0, 2, 1), left_ids[:, :, None], right_ids[:, :, None]], axis=2)
    return slot_table.reshape(LEAVES, SLOTS).astype(jnp.int32)


def draw_base_skeleton(key, part):
    key = jax.random.fold_in(key, 5)
    node_keys = jax.random.split(key, N_LEAF)
    return jax.vmap(lambda node_key: jax.random.permutation(node_key, LEAVES_DEV * LEAF)[:SKEL])(node_keys).astype(jnp.int32)


def draw_upper_skeleton(key, part):
    key = jax.random.fold_in(key, 6)

    def one_node(dev_no, level_no):
        group_no = dev_no >> level_no + 1
        node_key = jax.random.fold_in(jax.random.fold_in(key, level_no), group_no)
        return jax.random.permutation(node_key, 2 * SKEL)[:SKEL].astype(jnp.int32)
    devices = jnp.arange(N_LEAF, dtype=jnp.int32)
    level_ids = jnp.arange(LEVELS, dtype=jnp.int32)
    return jax.vmap(lambda dev_no: jax.vmap(lambda level_no: one_node(dev_no, level_no))(level_ids))(devices)


def transfer_values(key):

    def one_node(dev_no, level_no):
        group_no = dev_no >> level_no + 1
        node_key = jax.random.fold_in(jax.random.fold_in(key, level_no), group_no)
        key_normal = jax.random.fold_in(node_key, 0)
        normal_part = jnp.clip(jax.random.normal(key_normal, (2 * SKEL, SKEL)), -4.0, 4.0)
        return normal_part / math.sqrt(2 * SKEL)
    devices = jnp.arange(N_LEAF, dtype=jnp.int32)
    level_ids = jnp.arange(LEVELS, dtype=jnp.int32)
    return jax.vmap(lambda dev_no: jax.vmap(lambda level_no: one_node(dev_no, level_no))(level_ids))(devices)


def draw_transfer(key, part):
    key = jax.random.fold_in(key, 7)
    return transfer_values(key).astype(jnp.float32)


def block_levels(stream_key, shape, shards, least, largest):
    loudness, own = 1.0, jax.random.fold_in(stream_key, 6)
    for position, shards_of in shards:
        heights = jnp.exp(jax.random.uniform(jax.random.fold_in(own, position), (shards_of,), jnp.float32, least / len(shards), largest / len(shards)))
        loudness = loudness * jnp.repeat(heights, shape[position] // shards_of).reshape([-1 if axis == position else 1 for axis in range(len(shape))])
    return loudness


def noise(key, extent, deviation, limit, pieces=(), held_as=jnp.bfloat16):
    array = jax.random.normal(key, extent, jnp.float32) * deviation
    if len(pieces) > 0:
        array = block_levels(key, extent, pieces, -0.22, 0.18) * array
    return jnp.clip(array, min=-limit, max=limit).astype(held_as)


def setup_inputs(seed: int = 0) -> dict:
    splits = jax.random.split(jax.random.key(seed), 10)
    return {
        "features": draw_features(jax.random.fold_in(splits[9], 71), 0),
        "solution": noise(splits[1], (NRHS, POINTS), 1.0, 6.0, ((1, 256),), jnp.float32),
        "residual": draw_residual(jax.random.fold_in(splits[9], 71), 0),
        "direction": draw_direction(jax.random.fold_in(splits[9], 71), 0),
        "neighbours": draw_neighbours(jax.random.fold_in(splits[9], 71), 0),
        "skeleton_basis": noise(splits[5], (SKEL, POINTS), (LEAVES_DEV * LEAF) ** -0.5, 0.09375, ((1, 256),), jnp.float32),
        "base_skeleton": draw_base_skeleton(jax.random.fold_in(splits[9], 71), 0),
        "upper_skeleton": draw_upper_skeleton(jax.random.fold_in(splits[9], 71), 0),
        "transfer": draw_transfer(jax.random.fold_in(splits[9], 71), 0),
    }


HIGHEST = lax.Precision.HIGHEST
ridge_scale = 1.0
kernel_width = 8.0
near_weight = 0.125


def kernel_matrix(source, target):
    inner_prod = jnp.dot(source.T, target, precision=HIGHEST, preferred_element_type=jnp.float32)
    source_sq = jnp.sum(source * source, axis=0)
    target_sq = jnp.sum(target * target, axis=0)
    return jnp.exp(-(source_sq[:, None] + target_sq[None, :] - 2.0 * inner_prod) / kernel_width)


def rounded_copy(values):
    return lax.optimization_barrier(values.astype(jnp.bfloat16)).astype(jnp.float32)


def near_part(features, direction, neighbours):
    leaf_total = neighbours.shape[0]
    near_points = rounded_copy(features).reshape(DIM, leaf_total, LEAF).transpose(1, 0, 2)
    near_values = rounded_copy(direction).reshape(NRHS, leaf_total, LEAF).transpose(1, 0, 2)

    def one_leaf(leaf_no):
        own_points = near_points[leaf_no]
        own_tile = rounded_copy(kernel_matrix(own_points, own_points))
        own_term = jnp.dot(near_values[leaf_no], own_tile, precision=HIGHEST, preferred_element_type=jnp.float32)
        partner = neighbours[leaf_no]
        filled = partner >= 0
        safe_id = jnp.where(filled, partner, 0)
        partner_points = near_points[safe_id]
        partner_values = near_values[safe_id] * filled.astype(jnp.float32)[:, None, None]
        partner_tiles = rounded_copy(jax.vmap(kernel_matrix, in_axes=(0, None))(partner_points, own_points))
        partner_term = jnp.einsum("srj,sji->ri", partner_values, partner_tiles, precision=HIGHEST)
        return own_term + near_weight * partner_term

    device_leaves = jnp.arange(leaf_total, dtype=jnp.int32).reshape(-1, LEAVES_DEV)
    terms = lax.map(jax.vmap(one_leaf), device_leaves)
    terms = terms.reshape(leaf_total, NRHS, LEAF)
    return terms.transpose(1, 0, 2).reshape(NRHS, leaf_total * LEAF)


def far_part(features, direction, skeleton_basis, base_skeleton, upper_skeleton, transfer):
    nodes = base_skeleton.shape[0]
    node_points = direction.shape[1] // nodes
    node_dir = direction.reshape(NRHS, nodes, node_points)
    node_basis = skeleton_basis.reshape(SKEL, nodes, node_points)
    node_feat = features.reshape(DIM, nodes, node_points)
    weights = jnp.einsum("snd,rnd->nsr", node_basis, node_dir, precision=HIGHEST)
    points = jax.vmap(lambda feat_block, chosen: jnp.take(feat_block, chosen, axis=1), in_axes=(1, 0))(node_feat, base_skeleton)
    level_weights = [weights]
    level_points = [points]
    for level in range(LEVELS):
        parents = weights.shape[0] // 2
        span = 2 ** (level + 1)
        stacked = weights.reshape(parents, 2 * SKEL, NRHS)
        paired = points.reshape(parents, 2, DIM, SKEL).transpose(0, 2, 1, 3).reshape(parents, DIM, 2 * SKEL)
        matrices = transfer[::span, level]
        selection = upper_skeleton[::span, level]
        weights = jnp.einsum("gks,gkr->gsr", matrices, stacked, precision=HIGHEST)
        points = jax.vmap(lambda pair_block, chosen: jnp.take(pair_block, chosen, axis=1))(paired, selection)
        level_weights.append(weights)
        level_points.append(points)
    couplings = []
    for level in range(LEVELS + 1):
        kernels = jax.vmap(kernel_matrix)(level_points[level], level_points[level])
        couplings.append(jnp.einsum("nst,ntr->nsr", kernels, level_weights[level], precision=HIGHEST))
    descent = couplings[LEVELS]
    for level in reversed(range(LEVELS)):
        span = 2 ** (level + 1)
        matrices = transfer[::span, level]
        spread = jnp.einsum("gks,gsr->gkr", matrices, descent, precision=HIGHEST)
        descent = couplings[level] + spread.reshape(-1, SKEL, NRHS)
    far_field = jnp.einsum("nsr,snd->rnd", descent, node_basis, precision=HIGHEST)
    return far_field.reshape(NRHS, nodes * node_points)


def reference(features, solution, residual, direction, neighbours, skeleton_basis, base_skeleton, upper_skeleton, transfer):
    near_field = near_part(features, direction, neighbours)
    far_field = far_part(features, direction, skeleton_basis, base_skeleton, upper_skeleton, transfer)
    image = ridge_scale * direction + near_field + far_field
    norm_old = jnp.sum(residual * residual, axis=1)
    curvature = jnp.sum(direction * image, axis=1)
    step_size = norm_old / curvature
    new_solution = solution + step_size[:, None] * direction
    new_residual = residual - step_size[:, None] * image
    norm_new = jnp.sum(new_residual * new_residual, axis=1)
    new_direction = new_residual + (norm_new / norm_old)[:, None] * direction
    return (new_solution, new_residual, new_direction)
```

```python
import functools

import jax
import jax.numpy as jnp
from jax import lax
from jax.experimental import pallas as pl
from jax.experimental.pallas import tpu as pltpu
from jax.sharding import PartitionSpec as P

f32 = jnp.float32
bf16 = jnp.bfloat16
MESH = pl.DeviceIdType.MESH
NN = (((1,), (0,)), ((), ()))
NT = (((1,), (1,)), ((), ()))

LEVELS = 8
GROUP = 16
LEAVES = 16
WIDTH = 256
INNER = 6
BOUND = 4
RANK = 128
CLASSES = 64
DIMS = 8
CHUNK = 512
MASKS = (1, 2, 4, 14, 16, 48, 64, 192)
SHARE = (0, 2, 4, 4, 3, 3, 0, 0)


def flip(me, mask):
    out = me
    for bit in range(LEVELS):
        if mask >> bit & 1:
            out = out + (1 - 2 * (me // 2**bit % 2)) * 2**bit
    return out


def dot(a, b, dims=NN):
    return lax.dot_general(a, b, dims, preferred_element_type=f32)


def split2(x):
    high = x.astype(bf16)
    return high, (x - high.astype(f32)).astype(bf16)


def split3(x):
    high = x.astype(bf16).astype(f32)
    rest = x - high
    mid = rest.astype(bf16).astype(f32)
    return high, mid, (rest - mid).astype(bf16).astype(f32)


def dot3(a, b, dims=NN):
    (ah, al), (bh, bl) = a, b
    rows = ah.shape[0]
    both = dot(jnp.concatenate([ah, al], axis=0), bh, dims)
    return both[:rows] + both[rows:] + dot(ah, bl, dims)


def norm_rows(norm, scale, swapped):
    high, mid, low = split3(norm)
    shape = (8, norm.shape[1])
    row = lax.broadcasted_iota(jnp.int32, shape, 0)
    first = 3 if swapped else 0
    ones = 0 if swapped else 3
    out = jnp.where((row >= ones) & (row < ones + 3), 1.0, 0.0).astype(f32)
    for i, piece in enumerate((high, mid, low)):
        out = jnp.where(row == first + i, jnp.broadcast_to(piece, shape), out)
    return out * scale


def gaussian(points):
    h, m, l = split3(points)
    norm = jnp.sum(points * points, axis=0, keepdims=True)
    pad = jnp.zeros_like(points)
    left = jnp.concatenate([h, h, m, h, m, l, norm_rows(norm, 1.0, False), pad], axis=0)
    right = jnp.concatenate(
        [0.25 * h, 0.25 * m, 0.25 * h, 0.25 * l, 0.25 * m, 0.25 * h, norm_rows(norm, -0.125, True), pad],
        axis=0,
    )
    return jnp.exp(dot(left.T.astype(bf16), right.astype(bf16)))


def pick(points, chosen):
    h, m, l = split3(points)
    stack = jnp.concatenate([h, m, l, jnp.zeros_like(h)], axis=0).astype(bf16)
    out = dot(stack, chosen)
    return (out[0:8] + out[8:16]) + out[16:24]


def one_hot(index_row, start, rows):
    at = lax.broadcasted_iota(jnp.int32, (rows, index_row.shape[1]), 0) + start
    return jnp.where(at == index_row, 1.0, 0.0).astype(bf16)


def kernel(
    nbr, base_ref, upper_ref, feat_ref, dir_any, res_any, basis_any, trans_any,
    nr_ref, ab_ref,
    dir_v, res_v, basis_v, trans_v, basis_h, basis_l, trans_h, trans_l, hots,
    source_v, target_v, value_v, near_v, edge_v, pos_s,
    tree_out, tree_in, halo_out, halo_in, lo_out, lo_in, hi_out, hi_in,
    local_sem, tree_s, tree_r, halo_s, halo_r, lo_s, lo_r, hi_s, hi_r,
):
    me = lax.axis_index("leaf")
    lo_id = me % GROUP
    hi_id = me // GROUP
    halves = [me // 2**level % 2 for level in range(LEVELS)]

    copies = {}
    quarter = basis_v.shape[1] // 4
    copies["dir"] = pltpu.make_async_copy(dir_any, dir_v, local_sem.at[0])
    copies["dir"].start()
    for i in range(4):
        cols = pl.ds(i * quarter, quarter)
        copies[i] = pltpu.make_async_copy(basis_any.at[:, cols], basis_v.at[:, cols], local_sem.at[1 + i])
        copies[i].start()
    copies["trans"] = pltpu.make_async_copy(trans_any.at[0], trans_v, local_sem.at[5])
    copies["trans"].start()
    copies["res"] = pltpu.make_async_copy(res_any, res_v, local_sem.at[6])
    copies["res"].start()

    barrier = pltpu.get_barrier_semaphore()
    right = (me + 1) % 256
    left = (me + 255) % 256
    peers = [right, left]
    peers += [hi_id * GROUP + (lo_id + m) % GROUP for m in range(1, GROUP)]
    peers += [(me + GROUP * m) % 256 for m in range(1, GROUP)]
    for peer in peers:
        pl.semaphore_signal(barrier, inc=1, device_id=(peer,), device_id_type=MESH)

    edges = []
    for slot in (6, 7):
        count = jnp.int32(0)
        mine = [jnp.int32(0)] * BOUND
        theirs = [jnp.int32(0)] * BOUND
        for k in range(LEAVES):
            partner = nbr[k, slot]
            filled = partner >= 0
            place = jnp.minimum(count, BOUND - 1) + (BOUND + 1 if slot == 6 else 0)
            pos_s[slot - 6, k] = jnp.where(filled, place, BOUND)
            for q in range(BOUND):
                here = filled & (count == q)
                mine[q] = jnp.where(here, k, mine[q])
                theirs[q] = jnp.where(here, partner, theirs[q])
            count = count + filled.astype(jnp.int32)
        ranks = []
        for q in range(BOUND):
            rank = jnp.int32(0)
            for p in range(BOUND):
                if p != q:
                    rank = rank + (theirs[p] < theirs[q]).astype(jnp.int32)
            ranks.append(jnp.minimum(rank, BOUND - 1))
        edges.append((mine, ranks))

    points = jnp.zeros((32, RANK), f32)
    base_row = base_ref[...]
    for c in range(feat_ref.shape[1] // CHUNK):
        feat = feat_ref[:, c * CHUNK : (c + 1) * CHUNK]
        h, m, l = split3(feat)
        stack = jnp.concatenate([h, m, l, jnp.zeros_like(h)], axis=0).astype(bf16)
        points = points + dot(stack, one_hot(base_row, c * CHUNK, CHUNK))
        norm = jnp.sum(h * h, axis=0, keepdims=True)
        source = jnp.concatenate([h, norm_rows(norm, 1.0, False)], axis=0)
        target = jnp.concatenate([0.25 * h, norm_rows(norm, -0.125, True)], axis=0)
        for i in range(CHUNK // WIDTH):
            k = c * (CHUNK // WIDTH) + i
            block = source[:, i * WIDTH : (i + 1) * WIDTH]
            value_v[k, CLASSES:, :] = block.astype(bf16)
            source_v[k] = block.T.astype(bf16)
            target_v[k] = target[:, i * WIDTH : (i + 1) * WIDTH].astype(bf16)
    points = (points[0:8] + points[8:16]) + points[16:24]

    copies["dir"].wait()
    weights = jnp.zeros((CLASSES, RANK), f32)
    for c in range(dir_v.shape[1] // CHUNK):
        if c % (quarter // CHUNK) == 0:
            copies[c // (quarter // CHUNK)].wait()
        cols = slice(c * CHUNK, (c + 1) * CHUNK)
        dh, dl = split2(dir_v[:, cols])
        bh, bl = split2(basis_v[:, cols])
        basis_h[:, cols] = bh
        basis_l[:, cols] = bl
        for i in range(CHUNK // WIDTH):
            value_v[c * (CHUNK // WIDTH) + i, :CLASSES, :] = dh[:, i * WIDTH : (i + 1) * WIDTH]
        weights = weights + dot3((dh, dl), (bh, bl), NT)

    pl.semaphore_wait(barrier, len(peers))

    def tile(source, k):
        return jnp.exp(dot(source, target_v[k])).astype(bf16)

    def near_leaf(k, carry):
        own = dot(value_v[k, :CLASSES, :], tile(source_v[k], k))
        sides = jnp.zeros((CLASSES, WIDTH), f32)
        for s in range(INNER):
            partner = nbr[k, s]
            filled = partner >= 0
            j = jnp.clip(partner - me * LEAVES, 0, LEAVES - 1)
            scale = jnp.where(filled, 0.125, 0.0).astype(f32)
            sides = sides + scale * dot(value_v[j, :CLASSES, :], tile(source_v[j], k))
        near_v[k] = own + sides
        return carry

    def near_edge(side, at):
        mine, ranks = edges[side]
        for q in range(BOUND):
            block = halo_in[side, ranks[q]]
            source = block[CLASSES:].astype(f32).T.astype(bf16)
            edge_v[at + q] = 0.125 * dot(block[:CLASSES], tile(source, mine[q]))

    def lane_sums(x):
        out = x[:, :RANK]
        for i in range(1, x.shape[1] // RANK):
            out = out + x[:, i * RANK : (i + 1) * RANK]
        return out

    def as_row(top, bottom):
        return jnp.sum(jnp.concatenate([top, bottom], axis=0).T, axis=0, keepdims=True)

    def as_columns(row):
        return jnp.broadcast_to(row, (RANK, RANK)).T

    def spread(row, out, into, sems, recvs, use, own_id, where):
        out[use] = row
        into[use, own_id] = row
        started = []
        for m in range(1, GROUP):
            peer, slot = where(m)
            send = pltpu.make_async_remote_copy(
                src_ref=out.at[use], dst_ref=into.at[use, own_id],
                send_sem=sems.at[use, m], recv_sem=recvs.at[use, own_id],
                device_id=(peer,), device_id_type=MESH,
            )
            send.start()
            arrival = pltpu.make_async_remote_copy(
                src_ref=out.at[use], dst_ref=into.at[use, slot],
                send_sem=sems.at[use, m], recv_sem=recvs.at[use, slot],
                device_id=(peer,), device_id_type=MESH,
            )
            started.append((send, arrival))
        return started

    def lo_peer(m):
        slot = (lo_id + m) % GROUP
        return hi_id * GROUP + slot, slot

    def hi_peer(m):
        slot = (hi_id + m) % GROUP
        return slot * GROUP + lo_id, slot

    def total(started, into, use):
        for _, arrival in started:
            arrival.wait_recv()
        return jnp.sum(into[use], axis=0)

    sent = []
    lo_first = hi_first = None
    halo_copies = []
    done = 0
    matrix = None
    descent = None
    quad = jnp.zeros((CLASSES, RANK), f32)
    group_quad = jnp.zeros((CLASSES, RANK), f32)
    for level in range(LEVELS):
        tree_out[level, :CLASSES] = weights
        tree_out[level, CLASSES:] = points
        message = pltpu.make_async_remote_copy(
            src_ref=tree_out.at[level], dst_ref=tree_in.at[level],
            send_sem=tree_s.at[level], recv_sem=tree_r.at[level],
            device_id=(flip(me, MASKS[level]),), device_id_type=MESH,
        )
        message.start()
        sent.append(message)
        if level == 0:
            copies["trans"].wait()
            for i in range(LEVELS):
                th, tl = split2(trans_v[i])
                trans_h[i] = th
                trans_l[i] = tl
                hots[i] = one_hot(upper_ref[0, i : i + 1, :], 0, 2 * RANK)
        half = halves[level]
        mine = pl.ds(pl.multiple_of(half * RANK, RANK), RANK)
        other = pl.ds(pl.multiple_of((1 - half) * RANK, RANK), RANK)
        step = (trans_h[level, mine], trans_l[level, mine])
        part = dot3(split2(weights), step)
        if level == 0:
            for side, target in ((0, left), (1, right)):
                leaves = edges[side][0]
                for q in range(BOUND):
                    halo_out[side, q] = value_v[leaves[q]]
                halo = pltpu.make_async_remote_copy(
                    src_ref=halo_out.at[side], dst_ref=halo_in.at[1 - side],
                    send_sem=halo_s.at[side], recv_sem=halo_r.at[1 - side],
                    device_id=(target,), device_id_type=MESH,
                )
                halo.start()
                halo_copies.append(halo)
        couple = dot3(split2(weights), split2(gaussian(points)))
        if level == 0:
            descent = couple
        else:
            descent = descent + dot3(split2(couple), matrix, NT)
        if level < 4:
            quad = quad + 0.5**level * (weights * couple)
        else:
            group_quad = group_quad + 0.5 ** (level - 4) * (weights * couple)
        if level == 0:
            matrix = step
        else:
            matrix = split2(dot3(matrix, step))
        if SHARE[level]:
            lax.fori_loop(done, done + SHARE[level], near_leaf, 0)
            done += SHARE[level]
        if level == 3:
            halo_copies[0].wait_recv()
            halo_copies[1].wait_recv()
            edge_v[4] = jnp.zeros((CLASSES, WIDTH), f32)
            near_edge(1, 0)
            near_edge(0, 5)
        if level == 6:
            copies["res"].wait()

            def finish_leaf(k, carry):
                curve, norm = carry
                cols = pl.ds(pl.multiple_of(k * WIDTH, WIDTH), WIDTH)
                d = dir_v[:, cols]
                near = d + (near_v[k] + (edge_v[pos_s[0, k]] + edge_v[pos_s[1, k]]))
                near_v[k] = near
                r = res_v[:, cols]
                return curve + lane_sums(d * near), norm + lane_sums(r * r)

            zero = jnp.zeros((CLASSES, RANK), f32)
            curve, norm = lax.fori_loop(0, LEAVES, finish_leaf, (zero, zero))
            lo_first = spread(as_row(curve + quad, norm), lo_out, lo_in, lo_s, lo_r, 0, lo_id, lo_peer)
        if level == 7:
            row = total(lo_first, lo_in, 0)
            row = row + as_row(group_quad, jnp.zeros_like(group_quad))
            hi_first = spread(row, hi_out, hi_in, hi_s, hi_r, 0, hi_id, hi_peer)
        message.wait_recv()
        weights = part + dot3(split2(tree_in[level, :CLASSES]), (trans_h[level, other], trans_l[level, other]))
        theirs = tree_in[level, CLASSES:]
        low = jnp.where(half == 1, theirs, points)
        high = jnp.where(half == 1, points, theirs)
        points = pick(jnp.concatenate([low, high], axis=1), hots[level])

    couple = dot3(split2(weights), split2(gaussian(points)))
    descent = descent + dot3(split2(couple), matrix, NT)
    top = as_row(weights * couple, jnp.zeros_like(couple))
    dh, dl = split2(descent)
    both = jnp.concatenate([dh, dl], axis=0)

    row = total(hi_first, hi_in, 0) + top
    sums = as_columns(row)
    norm_old = sums[CLASSES:]
    step_size = norm_old / sums[:CLASSES]
    wide_step = jnp.concatenate([step_size, step_size], axis=1)

    def update(k, norm):
        cols = pl.ds(pl.multiple_of(k * WIDTH, WIDTH), WIDTH)
        bh = basis_h[:, cols]
        far = dot(both, bh)
        far = far[:CLASSES] + far[CLASSES:] + dot(dh, basis_l[:, cols])
        new = res_v[:, cols] - wide_step * (near_v[k] + far)
        nr_ref[:, cols] = new
        return norm + lane_sums(new * new)

    norm = lax.fori_loop(0, LEAVES, update, jnp.zeros((CLASSES, RANK), f32))
    row = as_row(norm, jnp.zeros_like(norm))
    lo_second = spread(row, lo_out, lo_in, lo_s, lo_r, 1, lo_id, lo_peer)
    row = total(lo_second, lo_in, 1)
    hi_second = spread(row, hi_out, hi_in, hi_s, hi_r, 1, hi_id, hi_peer)
    row = total(hi_second, hi_in, 1)
    ab_ref[0] = step_size
    ab_ref[1] = as_columns(row)[:CLASSES] / norm_old

    for message in sent + halo_copies:
        message.wait_send()
    for started in (lo_first, hi_first, lo_second, hi_second):
        for send, _ in started:
            send.wait_send()


def on_device(
    features, solution, residual, direction, neighbours,
    skeleton_basis, base_skeleton, upper_skeleton, transfer,
):
    classes, points = direction.shape
    vmem = pl.BlockSpec(memory_space=pltpu.VMEM)
    whole = pl.BlockSpec(memory_space=pl.ANY)
    dma = pltpu.SemaphoreType.DMA
    new_residual, factors = pl.pallas_call(
        kernel,
        out_shape=(
            jax.ShapeDtypeStruct((classes, points), f32),
            jax.ShapeDtypeStruct((2, classes, RANK), f32),
        ),
        in_specs=[pl.BlockSpec(memory_space=pltpu.SMEM), vmem, vmem, vmem, whole, whole, whole, whole],
        out_specs=(vmem, vmem),
        scratch_shapes=[
            pltpu.VMEM((classes, points), f32),
            pltpu.VMEM((classes, points), f32),
            pltpu.VMEM((RANK, points), f32),
            pltpu.VMEM((LEVELS, 2 * RANK, RANK), f32),
            pltpu.VMEM((RANK, points), bf16),
            pltpu.VMEM((RANK, points), bf16),
            pltpu.VMEM((LEVELS, 2 * RANK, RANK), bf16),
            pltpu.VMEM((LEVELS, 2 * RANK, RANK), bf16),
            pltpu.VMEM((LEVELS, 2 * RANK, RANK), bf16),
            pltpu.VMEM((LEAVES, WIDTH, 16), bf16),
            pltpu.VMEM((LEAVES, 16, WIDTH), bf16),
            pltpu.VMEM((LEAVES, CLASSES + 16, WIDTH), bf16),
            pltpu.VMEM((LEAVES, CLASSES, WIDTH), f32),
            pltpu.VMEM((9, CLASSES, WIDTH), f32),
            pltpu.SMEM((2, LEAVES), jnp.int32),
            pltpu.VMEM((LEVELS, CLASSES + DIMS, RANK), f32),
            pltpu.VMEM((LEVELS, CLASSES + DIMS, RANK), f32),
            pltpu.VMEM((2, BOUND, CLASSES + 16, WIDTH), bf16),
            pltpu.VMEM((2, BOUND, CLASSES + 16, WIDTH), bf16),
            pltpu.VMEM((2, 1, RANK), f32),
            pltpu.VMEM((2, GROUP, 1, RANK), f32),
            pltpu.VMEM((2, 1, RANK), f32),
            pltpu.VMEM((2, GROUP, 1, RANK), f32),
            dma((7,)),
            dma((LEVELS,)),
            dma((LEVELS,)),
            dma((2,)),
            dma((2,)),
            dma((2, GROUP)),
            dma((2, GROUP)),
            dma((2, GROUP)),
            dma((2, GROUP)),
        ],
        compiler_params=pltpu.CompilerParams(
            collective_id=0, has_side_effects=True, vmem_limit_bytes=40 * 1024 * 1024
        ),
        name="cg_step",
    )(neighbours, base_skeleton, upper_skeleton, features, direction, residual, skeleton_basis, transfer)
    step_size = factors[0, :, :1]
    ratio = factors[1, :, :1]
    new_solution = solution + step_size * direction
    new_direction = new_residual + ratio * direction
    return (new_solution, new_residual, new_direction)


def solution(mesh):
    placed = (
        P(None, "leaf"),
        P(None, "leaf"),
        P(None, "leaf"),
        P(None, "leaf"),
        P("leaf", None),
        P(None, "leaf"),
        P("leaf", None),
        P("leaf", None, None),
        P("leaf", None, None, None),
    )
    return jax.shard_map(
        on_device,
        mesh=mesh,
        in_specs=placed,
        out_specs=(P(None, "leaf"), P(None, "leaf"), P(None, "leaf")),
        check_vma=False,
    )
```

```python
import functools

import jax
import jax.numpy as jnp
from jax import lax
from jax.experimental import pallas as pl
from jax.experimental.pallas import tpu as pltpu
from jax.sharding import PartitionSpec as P

f32 = jnp.float32
bf16 = jnp.bfloat16
MESH = pl.DeviceIdType.MESH
NN = (((1,), (0,)), ((), ()))
NT = (((1,), (1,)), ((), ()))

LEVELS = 8
GROUP = 16
LEAVES = 16
WIDTH = 256
INNER = 6
BOUND = 4
RANK = 128
CLASSES = 64
DIMS = 8
CHUNK = 512
FINISH = 1024
MASKS = (1, 2, 4, 14, 16, 48, 64, 192)
TEAM = 4
TILES = INNER + 1
STEPS = LEAVES // TEAM * TILES // 2
SHARE = (0, 2, 3, 4, 3, 2, 0, 0)


def flip(me, mask):
    out = me
    for bit in range(LEVELS):
        if mask >> bit & 1:
            out = out + (1 - 2 * (me // 2**bit % 2)) * 2**bit
    return out


def dot(a, b, dims=NN):
    return lax.dot_general(a, b, dims, preferred_element_type=f32)


def split2(x):
    high = x.astype(bf16)
    return high, (x - high.astype(f32)).astype(bf16)


def split3(x):
    high = x.astype(bf16).astype(f32)
    rest = x - high
    mid = rest.astype(bf16).astype(f32)
    return high, mid, (rest - mid).astype(bf16).astype(f32)


def dot3(a, b, dims=NN):
    (ah, al), (bh, bl) = a, b
    rows = ah.shape[0]
    both = dot(jnp.concatenate([ah, al], axis=0), bh, dims)
    return both[:rows] + both[rows:] + dot(ah, bl, dims)


def norm_rows(norm, scale, swapped):
    high, mid, low = split3(norm)
    shape = (8, norm.shape[1])
    row = lax.broadcasted_iota(jnp.int32, shape, 0)
    first = 3 if swapped else 0
    ones = 0 if swapped else 3
    out = jnp.where((row >= ones) & (row < ones + 3), 1.0, 0.0).astype(f32)
    for i, piece in enumerate((high, mid, low)):
        out = jnp.where(row == first + i, jnp.broadcast_to(piece, shape), out)
    return out * scale


def gaussian(points):
    h, m, l = split3(points)
    norm = jnp.sum(points * points, axis=0, keepdims=True)
    pad = jnp.zeros_like(points)
    left = jnp.concatenate([h, h, m, h, m, l, norm_rows(norm, 1.0, False), pad], axis=0)
    right = jnp.concatenate(
        [0.25 * h, 0.25 * m, 0.25 * h, 0.25 * l, 0.25 * m, 0.25 * h, norm_rows(norm, -0.125, True), pad],
        axis=0,
    )
    return jnp.exp(dot(left.T.astype(bf16), right.astype(bf16)))


def pick(points, chosen):
    h, m, l = split3(points)
    stack = jnp.concatenate([h, m, l, jnp.zeros_like(h)], axis=0).astype(bf16)
    out = dot(stack, chosen)
    return (out[0:8] + out[8:16]) + out[16:24]


def one_hot(index_row, start, rows):
    at = lax.broadcasted_iota(jnp.int32, (rows, index_row.shape[1]), 0) + start
    return jnp.where(at == index_row, 1.0, 0.0).astype(bf16)


def kernel(
    nbr_any, base_ref, upper_ref, feat_ref, dir_any, res_any, basis_any, trans_any,
    nr_ref, ab_ref,
    dir_v, res_v, basis_v, trans_v, basis_h, basis_l, trans_h, trans_l, hots,
    source_v, target_v, value_v, near_v, edge_v, tile_v, nbr, pos_s,
    tree_out, tree_in, halo_out, halo_in, lo_out, lo_in, hi_out, hi_in,
    local_sem, tree_s, tree_r, halo_s, halo_r, lo_s, lo_r, hi_s, hi_r,
):
    me = lax.axis_index("leaf")
    lo_id = me % GROUP
    hi_id = me // GROUP
    halves = [me // 2**level % 2 for level in range(LEVELS)]

    copies = {}
    copies["nbr"] = pltpu.make_async_copy(nbr_any, nbr, local_sem.at[7])
    copies["nbr"].start()
    quarter = basis_v.shape[1] // 4
    copies["dir"] = pltpu.make_async_copy(dir_any, dir_v, local_sem.at[0])
    copies["dir"].start()
    for i in range(4):
        cols = pl.ds(i * quarter, quarter)
        copies[i] = pltpu.make_async_copy(basis_any.at[:, cols], basis_v.at[:, cols], local_sem.at[1 + i])
        copies[i].start()
    copies["trans"] = pltpu.make_async_copy(trans_any.at[0], trans_v, local_sem.at[5])
    copies["trans"].start()
    copies["res"] = pltpu.make_async_copy(res_any, res_v, local_sem.at[6])
    copies["res"].start()

    barrier = pltpu.get_barrier_semaphore()
    right = (me + 1) % 256
    left = (me + 255) % 256
    peers = [right, left]
    peers += [hi_id * GROUP + (lo_id + m) % GROUP for m in range(1, GROUP)]
    peers += [(me + GROUP * m) % 256 for m in range(1, GROUP)]
    for peer in peers:
        pl.semaphore_signal(barrier, inc=1, device_id=(peer,), device_id_type=MESH)

    copies["nbr"].wait()
    edges = []
    for slot in (6, 7):
        count = jnp.int32(0)
        mine = [jnp.int32(0)] * BOUND
        theirs = [jnp.int32(0)] * BOUND
        for k in range(LEAVES):
            partner = nbr[k, slot]
            filled = partner >= 0
            place = jnp.minimum(count, BOUND - 1) + (BOUND + 1 if slot == 6 else 0)
            pos_s[slot - 6, k] = jnp.where(filled, place, BOUND)
            for q in range(BOUND):
                here = filled & (count == q)
                mine[q] = jnp.where(here, k, mine[q])
                theirs[q] = jnp.where(here, partner, theirs[q])
            count = count + filled.astype(jnp.int32)
        ranks = []
        for q in range(BOUND):
            rank = jnp.int32(0)
            for p in range(BOUND):
                if p != q:
                    rank = rank + (theirs[p] < theirs[q]).astype(jnp.int32)
            ranks.append(jnp.minimum(rank, BOUND - 1))
        edges.append((mine, ranks))

    points = jnp.zeros((32, RANK), f32)
    base_row = base_ref[...]
    for c in range(feat_ref.shape[1] // CHUNK):
        feat = feat_ref[:, c * CHUNK : (c + 1) * CHUNK]
        h, m, l = split3(feat)
        stack = jnp.concatenate([h, m, l, jnp.zeros_like(h)], axis=0).astype(bf16)
        points = points + dot(stack, one_hot(base_row, c * CHUNK, CHUNK))
        norm = jnp.sum(h * h, axis=0, keepdims=True)
        source = jnp.concatenate([h, norm_rows(norm, 1.0, False)], axis=0)
        target = jnp.concatenate([0.25 * h, norm_rows(norm, -0.125, True)], axis=0)
        for i in range(CHUNK // WIDTH):
            k = c * (CHUNK // WIDTH) + i
            block = source[:, i * WIDTH : (i + 1) * WIDTH]
            value_v[k, CLASSES:, :] = block.astype(bf16)
            source_v[k] = block.T.astype(bf16)
            target_v[k] = target[:, i * WIDTH : (i + 1) * WIDTH].astype(bf16)
    points = (points[0:8] + points[8:16]) + points[16:24]

    copies["dir"].wait()
    weights = jnp.zeros((CLASSES, RANK), f32)
    for c in range(dir_v.shape[1] // CHUNK):
        if c % (quarter // CHUNK) == 0:
            copies[c // (quarter // CHUNK)].wait()
        cols = slice(c * CHUNK, (c + 1) * CHUNK)
        dh, dl = split2(dir_v[:, cols])
        bh, bl = split2(basis_v[:, cols])
        basis_h[:, cols] = bh
        basis_l[:, cols] = bl
        for i in range(CHUNK // WIDTH):
            value_v[c * (CHUNK // WIDTH) + i, :CLASSES, :] = dh[:, i * WIDTH : (i + 1) * WIDTH]
        weights = weights + dot3((dh, dl), (bh, bl), NT)

    pl.semaphore_wait(barrier, len(peers))

    def tile(source, k):
        return jnp.exp(dot(source, target_v[k])).astype(bf16)

    def near_place(batch, member):
        slot = batch % TILES
        k = batch // TILES * TEAM + member
        partner = nbr[k, jnp.maximum(slot - 1, 0)]
        j = jnp.where(slot == 0, k, jnp.clip(partner - me * LEAVES, 0, LEAVES - 1))
        scale = jnp.where(slot == 0, 1.0, jnp.where(partner >= 0, 0.125, 0.0)).astype(f32)
        return k, j, scale

    def near_add(batch, buffer):
        for member in range(TEAM):
            k, j, scale = near_place(batch, member)
            near_v[k] = near_v[k] + scale * dot(value_v[j, :CLASSES, :], tile_v[buffer, member])

    def near_batch(batch, buffer):
        near_add(jnp.maximum(batch - 1, 0), 1 - buffer)
        for member in range(TEAM):
            k, j, _ = near_place(batch, member)
            tile_v[buffer, member] = tile(source_v[j], k)

    def near_step(step, carry):
        near_batch(2 * step, 0)
        near_batch(2 * step + 1, 1)
        return carry

    def near_edges():
        for side, at in ((1, 0), (0, 5)):
            mine, ranks = edges[side]
            for q in range(BOUND):
                source = halo_in[side, ranks[q], CLASSES:].astype(f32).T.astype(bf16)
                tile_v[side, q] = tile(source, mine[q])
        for side, at in ((1, 0), (0, 5)):
            ranks = edges[side][1]
            for q in range(BOUND):
                edge_v[at + q] = 0.125 * dot(halo_in[side, ranks[q], :CLASSES], tile_v[side, q])

    def lane_sums(x):
        out = x[:, :RANK]
        for i in range(1, x.shape[1] // RANK):
            out = out + x[:, i * RANK : (i + 1) * RANK]
        return out

    def as_row(top, bottom):
        return jnp.sum(jnp.concatenate([top, bottom], axis=0).T, axis=0, keepdims=True)

    def as_columns(row):
        return jnp.broadcast_to(row, (RANK, RANK)).T

    def spread(row, out, into, sems, recvs, use, own_id, where):
        out[use] = row
        into[use, own_id] = row
        started = []
        for m in range(1, GROUP):
            peer, slot = where(m)
            send = pltpu.make_async_remote_copy(
                src_ref=out.at[use], dst_ref=into.at[use, own_id],
                send_sem=sems.at[use, m], recv_sem=recvs.at[use, own_id],
                device_id=(peer,), device_id_type=MESH,
            )
            send.start()
            arrival = pltpu.make_async_remote_copy(
                src_ref=out.at[use], dst_ref=into.at[use, slot],
                send_sem=sems.at[use, m], recv_sem=recvs.at[use, slot],
                device_id=(peer,), device_id_type=MESH,
            )
            started.append((send, arrival))
        return started

    def lo_peer(m):
        slot = (lo_id + m) % GROUP
        return hi_id * GROUP + slot, slot

    def hi_peer(m):
        slot = (hi_id + m) % GROUP
        return slot * GROUP + lo_id, slot

    def total(started, into, use):
        for _, arrival in started:
            arrival.wait_recv()
        return jnp.sum(into[use], axis=0)

    sent = []
    lo_first = hi_first = None
    halo_copies = []
    done = 0
    matrix = None
    descent = None
    quad = jnp.zeros((CLASSES, RANK), f32)
    group_quad = jnp.zeros((CLASSES, RANK), f32)
    for level in range(LEVELS):
        tree_out[level, :CLASSES] = weights
        tree_out[level, CLASSES:] = points
        message = pltpu.make_async_remote_copy(
            src_ref=tree_out.at[level], dst_ref=tree_in.at[level],
            send_sem=tree_s.at[level], recv_sem=tree_r.at[level],
            device_id=(flip(me, MASKS[level]),), device_id_type=MESH,
        )
        message.start()
        sent.append(message)
        if level == 0:
            near_v[...] = jnp.zeros_like(near_v)
            tile_v[1] = jnp.zeros((TEAM, WIDTH, WIDTH), bf16)
            copies["trans"].wait()
            for i in range(LEVELS):
                th, tl = split2(trans_v[i])
                trans_h[i] = th
                trans_l[i] = tl
                hots[i] = one_hot(upper_ref[0, i : i + 1, :], 0, 2 * RANK)
        half = halves[level]
        mine = pl.ds(pl.multiple_of(half * RANK, RANK), RANK)
        other = pl.ds(pl.multiple_of((1 - half) * RANK, RANK), RANK)
        step = (trans_h[level, mine], trans_l[level, mine])
        part = dot3(split2(weights), step)
        if level == 0:
            for side, target in ((0, left), (1, right)):
                leaves = edges[side][0]
                for q in range(BOUND):
                    halo_out[side, q] = value_v[leaves[q]]
                halo = pltpu.make_async_remote_copy(
                    src_ref=halo_out.at[side], dst_ref=halo_in.at[1 - side],
                    send_sem=halo_s.at[side], recv_sem=halo_r.at[1 - side],
                    device_id=(target,), device_id_type=MESH,
                )
                halo.start()
                halo_copies.append(halo)
        couple = dot3(split2(weights), split2(gaussian(points)))
        if level == 0:
            descent = couple
        else:
            descent = descent + dot3(split2(couple), matrix, NT)
        if level < 4:
            quad = quad + 0.5**level * (weights * couple)
        else:
            group_quad = group_quad + 0.5 ** (level - 4) * (weights * couple)
        if level == 0:
            matrix = step
        else:
            matrix = split2(dot3(matrix, step))
        if SHARE[level]:
            lax.fori_loop(done, done + SHARE[level], near_step, 0)
            done += SHARE[level]
            if done == STEPS:
                near_add(2 * STEPS - 1, 1)
        if level == 5:
            halo_copies[0].wait_recv()
            halo_copies[1].wait_recv()
            edge_v[BOUND] = jnp.zeros((CLASSES, WIDTH), f32)
            near_edges()
        if level == 6:
            copies["res"].wait()

            def finish_leaf(k, carry):
                curve, norm = carry
                cols = pl.ds(pl.multiple_of(k * WIDTH, WIDTH), WIDTH)
                d = dir_v[:, cols]
                near = d + (near_v[k] + (edge_v[pos_s[0, k]] + edge_v[pos_s[1, k]]))
                near_v[k] = near
                r = res_v[:, cols]
                return curve + lane_sums(d * near), norm + lane_sums(r * r)

            zero = jnp.zeros((CLASSES, RANK), f32)
            curve, norm = lax.fori_loop(0, LEAVES, finish_leaf, (zero, zero))
            lo_first = spread(as_row(curve + quad, norm), lo_out, lo_in, lo_s, lo_r, 0, lo_id, lo_peer)
        if level == 7:
            row = total(lo_first, lo_in, 0)
            row = row + as_row(group_quad, jnp.zeros_like(group_quad))
            hi_first = spread(row, hi_out, hi_in, hi_s, hi_r, 0, hi_id, hi_peer)
        message.wait_recv()
        weights = part + dot3(split2(tree_in[level, :CLASSES]), (trans_h[level, other], trans_l[level, other]))
        theirs = tree_in[level, CLASSES:]
        low = jnp.where(half == 1, theirs, points)
        high = jnp.where(half == 1, points, theirs)
        points = pick(jnp.concatenate([low, high], axis=1), hots[level])

    couple = dot3(split2(weights), split2(gaussian(points)))
    descent = descent + dot3(split2(couple), matrix, NT)
    top = as_row(weights * couple, jnp.zeros_like(couple))
    dh, dl = split2(descent)
    both = jnp.concatenate([dh, dl], axis=0)

    def image(k, carry):
        cols = pl.ds(pl.multiple_of(k * WIDTH, WIDTH), WIDTH)
        far = dot(both, basis_h[:, cols])
        far = far[:CLASSES] + far[CLASSES:] + dot(dh, basis_l[:, cols])
        near_v[k] = near_v[k] + far
        return carry

    lax.fori_loop(0, LEAVES, image, 0, unroll=2)
    row = total(hi_first, hi_in, 0) + top
    sums = as_columns(row)
    norm_old = sums[CLASSES:]
    step_size = norm_old / sums[:CLASSES]
    wide_step = jnp.concatenate([step_size, step_size], axis=1)

    def update(k, norm):
        cols = pl.ds(pl.multiple_of(k * WIDTH, WIDTH), WIDTH)
        new = res_v[:, cols] - wide_step * near_v[k]
        nr_ref[:, cols] = new
        return norm + lane_sums(new * new)

    norm = lax.fori_loop(0, LEAVES, update, jnp.zeros((CLASSES, RANK), f32))
    row = as_row(norm, jnp.zeros_like(norm))
    lo_second = spread(row, lo_out, lo_in, lo_s, lo_r, 1, lo_id, lo_peer)
    row = total(lo_second, lo_in, 1)
    hi_second = spread(row, hi_out, hi_in, hi_s, hi_r, 1, hi_id, hi_peer)
    row = total(hi_second, hi_in, 1)
    ab_ref[0] = step_size
    ab_ref[1] = as_columns(row)[:CLASSES] / norm_old

    for message in sent + halo_copies:
        message.wait_send()
    for started in (lo_first, hi_first, lo_second, hi_second):
        for send, _ in started:
            send.wait_send()


def finish(factors, sol_ref, nr_ref, dir_ref, new_sol_ref, new_res_ref, new_dir_ref):
    wide = lambda x: jnp.concatenate([x] * (FINISH // RANK), axis=1)
    d = dir_ref[...]
    nr = nr_ref[...]
    new_sol_ref[...] = sol_ref[...] + wide(factors[0]) * d
    new_res_ref[...] = nr
    new_dir_ref[...] = nr + wide(factors[1]) * d


def on_device(
    features, solution, residual, direction, neighbours,
    skeleton_basis, base_skeleton, upper_skeleton, transfer,
):
    classes, points = direction.shape
    vmem = pl.BlockSpec(memory_space=pltpu.VMEM)
    whole = pl.BlockSpec(memory_space=pl.ANY)
    dma = pltpu.SemaphoreType.DMA
    new_residual, factors = pl.pallas_call(
        kernel,
        out_shape=(
            jax.ShapeDtypeStruct((classes, points), f32),
            jax.ShapeDtypeStruct((2, classes, RANK), f32),
        ),
        in_specs=[whole, vmem, vmem, vmem, whole, whole, whole, whole],
        out_specs=(vmem, vmem),
        scratch_shapes=[
            pltpu.VMEM((classes, points), f32),
            pltpu.VMEM((classes, points), f32),
            pltpu.VMEM((RANK, points), f32),
            pltpu.VMEM((LEVELS, 2 * RANK, RANK), f32),
            pltpu.VMEM((RANK, points), bf16),
            pltpu.VMEM((RANK, points), bf16),
            pltpu.VMEM((LEVELS, 2 * RANK, RANK), bf16),
            pltpu.VMEM((LEVELS, 2 * RANK, RANK), bf16),
            pltpu.VMEM((LEVELS, 2 * RANK, RANK), bf16),
            pltpu.VMEM((LEAVES, WIDTH, 16), bf16),
            pltpu.VMEM((LEAVES, 16, WIDTH), bf16),
            pltpu.VMEM((LEAVES, CLASSES + 16, WIDTH), bf16),
            pltpu.VMEM((LEAVES, CLASSES, WIDTH), f32),
            pltpu.VMEM((9, CLASSES, WIDTH), f32),
            pltpu.VMEM((2, TEAM, WIDTH, WIDTH), bf16),
            pltpu.SMEM((LEAVES, 8), jnp.int32),
            pltpu.SMEM((2, LEAVES), jnp.int32),
            pltpu.VMEM((LEVELS, CLASSES + DIMS, RANK), f32),
            pltpu.VMEM((LEVELS, CLASSES + DIMS, RANK), f32),
            pltpu.VMEM((2, BOUND, CLASSES + 16, WIDTH), bf16),
            pltpu.VMEM((2, BOUND, CLASSES + 16, WIDTH), bf16),
            pltpu.VMEM((2, 1, RANK), f32),
            pltpu.VMEM((2, GROUP, 1, RANK), f32),
            pltpu.VMEM((2, 1, RANK), f32),
            pltpu.VMEM((2, GROUP, 1, RANK), f32),
            dma((8,)),
            dma((LEVELS,)),
            dma((LEVELS,)),
            dma((2,)),
            dma((2,)),
            dma((2, GROUP)),
            dma((2, GROUP)),
            dma((2, GROUP)),
            dma((2, GROUP)),
        ],
        compiler_params=pltpu.CompilerParams(
            collective_id=0, has_side_effects=True, vmem_limit_bytes=60 * 1024 * 1024
        ),
        name="cg_step",
    )(neighbours, base_skeleton, upper_skeleton, features, direction, residual, skeleton_basis, transfer)
    block = pl.BlockSpec((classes, FINISH), lambda i: (0, i))
    return pl.pallas_call(
        finish,
        grid=(points // FINISH,),
        out_shape=[jax.ShapeDtypeStruct((classes, points), f32)] * 3,
        in_specs=[pl.BlockSpec((2, classes, RANK), lambda i: (0, 0, 0)), block, block, block],
        out_specs=[block] * 3,
        name="cg_finish",
    )(factors, solution, new_residual, direction)


def solution(mesh):
    placed = (
        P(None, "leaf"),
        P(None, "leaf"),
        P(None, "leaf"),
        P(None, "leaf"),
        P("leaf", None),
        P(None, "leaf"),
        P("leaf", None),
        P("leaf", None, None),
        P("leaf", None, None, None),
    )
    return jax.shard_map(
        on_device,
        mesh=mesh,
        in_specs=placed,
        out_specs=(P(None, "leaf"), P(None, "leaf"), P(None, "leaf")),
        check_vma=False,
    )
```

```python
import functools

import jax
import jax.numpy as jnp
from jax import lax
from jax.experimental import pallas as pl
from jax.experimental.pallas import tpu as pltpu
from jax.sharding import PartitionSpec as P

f32 = jnp.float32
bf16 = jnp.bfloat16
MESH = pl.DeviceIdType.MESH
NN = (((1,), (0,)), ((), ()))
NT = (((1,), (1,)), ((), ()))

LEVELS = 8
GROUP = 16
LEAVES = 16
WIDTH = 256
INNER = 6
BOUND = 4
RANK = 128
CLASSES = 64
DIMS = 8
CHUNK = 512
FINISH = 2048
STAGES = ((1,), (2, 4, 6), (14,), (16, 32, 48), (64, 128, 192))
FAR_FIRST = (8, 7, 9, 6, 10, 5, 11, 4, 12, 3, 13, 2, 14, 1, 15)
MESSAGES = sum(len(stage) for stage in STAGES)
TEAM = 4
TILES = INNER + 1
STEPS = LEAVES // TEAM * TILES // 2
SHARE = (0, 5, 4, 5, 0)


def flip(me, mask):
    out = me
    for bit in range(LEVELS):
        if mask >> bit & 1:
            out = out + (1 - 2 * (me // 2**bit % 2)) * 2**bit
    return out


def dot(a, b, dims=NN):
    return lax.dot_general(a, b, dims, preferred_element_type=f32)


def split2(x):
    high = x.astype(bf16)
    return high, (x - high.astype(f32)).astype(bf16)


def split3(x):
    high = x.astype(bf16).astype(f32)
    rest = x - high
    mid = rest.astype(bf16).astype(f32)
    return high, mid, (rest - mid).astype(bf16).astype(f32)


def dot3(a, b, dims=NN):
    (ah, al), (bh, bl) = a, b
    rows = ah.shape[0]
    both = dot(jnp.concatenate([ah, al], axis=0), bh, dims)
    return both[:rows] + both[rows:] + dot(ah, bl, dims)


def norm_rows(norm, scale, swapped):
    high, mid, low = split3(norm)
    shape = (8, norm.shape[1])
    row = lax.broadcasted_iota(jnp.int32, shape, 0)
    first = 3 if swapped else 0
    ones = 0 if swapped else 3
    out = jnp.where((row >= ones) & (row < ones + 3), 1.0, 0.0).astype(f32)
    for i, piece in enumerate((high, mid, low)):
        out = jnp.where(row == first + i, jnp.broadcast_to(piece, shape), out)
    return out * scale


def gaussian(points):
    h, m, l = split3(points)
    norm = jnp.sum(points * points, axis=0, keepdims=True)
    pad = jnp.zeros_like(points)
    left = jnp.concatenate([h, h, m, h, m, l, norm_rows(norm, 1.0, False), pad], axis=0)
    right = jnp.concatenate(
        [0.25 * h, 0.25 * m, 0.25 * h, 0.25 * l, 0.25 * m, 0.25 * h, norm_rows(norm, -0.125, True), pad],
        axis=0,
    )
    return jnp.exp(dot(left.T.astype(bf16), right.astype(bf16)))


def pick(points, chosen):
    h, m, l = split3(points)
    stack = jnp.concatenate([h, m, l, jnp.zeros_like(h)], axis=0).astype(bf16)
    out = dot(stack, chosen)
    return (out[0:8] + out[8:16]) + out[16:24]


def one_hot(index_row, start, rows):
    at = lax.broadcasted_iota(jnp.int32, (rows, index_row.shape[1]), 0) + start
    return jnp.where(at == index_row, 1.0, 0.0).astype(bf16)


def kernel(
    nbr_any, base_ref, upper_ref, feat_ref, dir_any, res_any, basis_any, trans_any,
    nr_ref, ab_ref,
    dir_v, res_v, basis_v, trans_v, basis_h, basis_l, trans_h, trans_l, hots,
    source_v, target_v, value_v, near_v, edge_v, tile_v, nbr, pos_s,
    node_v, descent_v, tree_out, tree_in, halo_out, halo_in, lo_out, lo_in, hi_out, hi_in,
    local_sem, tree_s, tree_r, halo_s, halo_r, lo_s, lo_r, hi_s, hi_r,
):
    me = lax.axis_index("leaf")
    lo_id = me % GROUP
    hi_id = me // GROUP
    halves = [me // 2**level % 2 for level in range(LEVELS)]

    copies = {}
    copies["nbr"] = pltpu.make_async_copy(nbr_any, nbr, local_sem.at[7])
    copies["nbr"].start()
    quarter = basis_v.shape[1] // 4
    copies["dir"] = pltpu.make_async_copy(dir_any, dir_v, local_sem.at[0])
    copies["dir"].start()
    for i in range(4):
        cols = pl.ds(i * quarter, quarter)
        copies[i] = pltpu.make_async_copy(basis_any.at[:, cols], basis_v.at[:, cols], local_sem.at[1 + i])
        copies[i].start()
    copies["trans"] = pltpu.make_async_copy(trans_any.at[0], trans_v, local_sem.at[5])
    copies["trans"].start()
    copies["res"] = pltpu.make_async_copy(res_any, res_v, local_sem.at[6])
    copies["res"].start()

    barrier = pltpu.get_barrier_semaphore()
    right = (me + 1) % 256
    left = (me + 255) % 256
    peers = [right, left]
    peers += [hi_id * GROUP + (lo_id + m) % GROUP for m in range(1, GROUP)]
    peers += [(me + GROUP * m) % 256 for m in range(1, GROUP)]
    for peer in peers:
        pl.semaphore_signal(barrier, inc=1, device_id=(peer,), device_id_type=MESH)

    copies["nbr"].wait()
    edges = []
    for slot in (6, 7):
        count = jnp.int32(0)
        mine = [jnp.int32(0)] * BOUND
        theirs = [jnp.int32(0)] * BOUND
        for k in range(LEAVES):
            partner = nbr[slot, k]
            filled = partner >= 0
            place = jnp.minimum(count, BOUND - 1) + (BOUND + 1 if slot == 6 else 0)
            pos_s[slot - 6, k] = jnp.where(filled, place, BOUND)
            for q in range(BOUND):
                here = filled & (count == q)
                mine[q] = jnp.where(here, k, mine[q])
                theirs[q] = jnp.where(here, partner, theirs[q])
            count = count + filled.astype(jnp.int32)
        ranks = []
        for q in range(BOUND):
            rank = jnp.int32(0)
            for p in range(BOUND):
                if p != q:
                    rank = rank + (theirs[p] < theirs[q]).astype(jnp.int32)
            ranks.append(jnp.minimum(rank, BOUND - 1))
        edges.append((mine, ranks))

    points = jnp.zeros((32, RANK), f32)
    base_row = base_ref[...]
    for c in range(feat_ref.shape[1] // CHUNK):
        feat = feat_ref[:, c * CHUNK : (c + 1) * CHUNK]
        h, m, l = split3(feat)
        stack = jnp.concatenate([h, m, l, jnp.zeros_like(h)], axis=0).astype(bf16)
        points = points + dot(stack, one_hot(base_row, c * CHUNK, CHUNK))
        norm = jnp.sum(h * h, axis=0, keepdims=True)
        source = jnp.concatenate([h, norm_rows(norm, 1.0, False)], axis=0)
        target = jnp.concatenate([0.25 * h, norm_rows(norm, -0.125, True)], axis=0)
        for i in range(CHUNK // WIDTH):
            k = c * (CHUNK // WIDTH) + i
            block = source[:, i * WIDTH : (i + 1) * WIDTH]
            value_v[k, CLASSES:, :] = block.astype(bf16)
            source_v[k] = block.T.astype(bf16)
            target_v[k] = target[:, i * WIDTH : (i + 1) * WIDTH].astype(bf16)
    points = (points[0:8] + points[8:16]) + points[16:24]

    copies["dir"].wait()
    weights = jnp.zeros((CLASSES, RANK), f32)
    for c in range(dir_v.shape[1] // CHUNK):
        if c % (quarter // CHUNK) == 0:
            copies[c // (quarter // CHUNK)].wait()
        cols = slice(c * CHUNK, (c + 1) * CHUNK)
        dh, dl = split2(dir_v[:, cols])
        bh, bl = split2(basis_v[:, cols])
        basis_h[:, cols] = bh
        basis_l[:, cols] = bl
        for i in range(CHUNK // WIDTH):
            value_v[c * (CHUNK // WIDTH) + i, :CLASSES, :] = dh[:, i * WIDTH : (i + 1) * WIDTH]
        weights = weights + dot3((dh, dl), (bh, bl), NT)

    pl.semaphore_wait(barrier, len(peers))

    def tile(source, k):
        return jnp.exp(dot(source, target_v[k])).astype(bf16)

    def near_place(batch, member):
        slot = batch % TILES
        k = batch // TILES * TEAM + member
        partner = nbr[jnp.maximum(slot - 1, 0), k]
        j = jnp.where(slot == 0, k, jnp.clip(partner - me * LEAVES, 0, LEAVES - 1))
        scale = jnp.where(slot == 0, 1.0, jnp.where(partner >= 0, 0.125, 0.0)).astype(f32)
        return k, j, scale

    def near_add(batch, buffer):
        for member in range(TEAM):
            k, j, scale = near_place(batch, member)
            near_v[k] = near_v[k] + scale * dot(value_v[j, :CLASSES, :], tile_v[buffer, member])

    def near_batch(batch, buffer):
        near_add(jnp.maximum(batch - 1, 0), 1 - buffer)
        for member in range(TEAM):
            k, j, _ = near_place(batch, member)
            tile_v[buffer, member] = tile(source_v[j], k)

    def near_step(step, carry):
        near_batch(2 * step, 0)
        near_batch(2 * step + 1, 1)
        return carry

    def near_edges():
        for side, at in ((1, 0), (0, 5)):
            mine, ranks = edges[side]
            for q in range(BOUND):
                source = halo_in[side, ranks[q], CLASSES:].astype(f32).T.astype(bf16)
                tile_v[side, q] = tile(source, mine[q])
        for side, at in ((1, 0), (0, 5)):
            ranks = edges[side][1]
            for q in range(BOUND):
                edge_v[at + q] = 0.125 * dot(halo_in[side, ranks[q], :CLASSES], tile_v[side, q])

    def lane_sums(x):
        out = x[:, :RANK]
        for i in range(1, x.shape[1] // RANK):
            out = out + x[:, i * RANK : (i + 1) * RANK]
        return out

    def as_row(top, bottom):
        return jnp.sum(jnp.concatenate([top, bottom], axis=0).T, axis=0, keepdims=True)

    def as_columns(row):
        return jnp.broadcast_to(row, (RANK, RANK)).T

    def spread(row, out, into, sems, recvs, use, own_id, where):
        out[use] = row
        into[use, own_id] = row
        started = []
        for m in FAR_FIRST:
            peer, slot = where(m)
            send = pltpu.make_async_remote_copy(
                src_ref=out.at[use], dst_ref=into.at[use, own_id],
                send_sem=sems.at[use, m], recv_sem=recvs.at[use, own_id],
                device_id=(peer,), device_id_type=MESH,
            )
            send.start()
            arrival = pltpu.make_async_remote_copy(
                src_ref=out.at[use], dst_ref=into.at[use, slot],
                send_sem=sems.at[use, m], recv_sem=recvs.at[use, slot],
                device_id=(peer,), device_id_type=MESH,
            )
            started.append((send, arrival))
        return started

    def lo_peer(m):
        slot = (lo_id + m) % GROUP
        return hi_id * GROUP + slot, slot

    def hi_peer(m):
        slot = (hi_id + m) % GROUP
        return slot * GROUP + lo_id, slot

    def total(started, into, use):
        for _, arrival in started:
            arrival.wait_recv()
        return jnp.sum(into[use], axis=0)

    def halo_start():
        started = []
        for side, target in ((0, left), (1, right)):
            leaves = edges[side][0]
            for q in range(BOUND):
                halo_out[side, q] = value_v[leaves[q]]
            halo = pltpu.make_async_remote_copy(
                src_ref=halo_out.at[side], dst_ref=halo_in.at[1 - side],
                send_sem=halo_s.at[side], recv_sem=halo_r.at[1 - side],
                device_id=(target,), device_id_type=MESH,
            )
            halo.start()
            started.append(halo)
        return started

    def split_level(level):
        th, tl = split2(trans_v[level])
        trans_h[level] = th
        trans_l[level] = tl
        hots[level] = one_hot(upper_ref[0, level : level + 1, :], 0, 2 * RANK)

    def raised(level, half, node):
        rows = pl.ds(pl.multiple_of(half * RANK, RANK), RANK)
        step = (trans_h[level, rows], trans_l[level, rows])
        return (
            dot3(split2(node[0]), step),
            pick(node[1], hots[level, rows]),
        )

    def plus(a, b):
        return (a[0] + b[0], a[1] + b[1])

    def keep(level, node):
        node_v[level, :CLASSES] = node[0]
        node_v[level, CLASSES:] = node[1]

    def coupled(level, matrix):
        weights = node_v[level, :CLASSES]
        couple = dot3(split2(weights), split2(gaussian(node_v[level, CLASSES:])))
        if level == 0:
            descent_v[0] = couple
            return None, weights * couple
        half = halves[level - 1]
        rows = pl.ds(pl.multiple_of(half * RANK, RANK), RANK)
        if level == 1:
            matrix = trans_v[0, rows]
        else:
            matrix = dot3(split2(matrix), (trans_h[level - 1, rows], trans_l[level - 1, rows]))
        descent_v[level] = dot3(split2(couple), split2(matrix.T))
        return matrix, weights * couple

    def finish_near():
        def finish_leaf(k, carry):
            curve, norm = carry
            cols = pl.ds(pl.multiple_of(k * WIDTH, WIDTH), WIDTH)
            d = dir_v[:, cols]
            near = d + (near_v[k] + (edge_v[pos_s[0, k]] + edge_v[pos_s[1, k]]))
            near_v[k] = near
            r = res_v[:, cols]
            return curve + lane_sums(d * near), norm + lane_sums(r * r)

        zero = jnp.zeros((CLASSES, RANK), f32)
        return lax.fori_loop(0, LEAVES, finish_leaf, (zero, zero))

    sent = []
    level = 0
    slot = 0
    done = 0
    node = (weights, points)
    keep(0, node)
    copies["trans"].wait()
    split_level(0)
    for stage, masks in enumerate(STAGES):
        gift = raised(level, halves[level], node)
        tree_out[stage, :CLASSES] = gift[0]
        tree_out[stage, CLASSES:] = gift[1]
        messages = []
        for mask in masks:
            message = pltpu.make_async_remote_copy(
                src_ref=tree_out.at[stage], dst_ref=tree_in.at[slot],
                send_sem=tree_s.at[slot], recv_sem=tree_r.at[slot],
                device_id=(flip(me, mask),), device_id_type=MESH,
            )
            message.start()
            messages.append((message, slot))
            slot += 1
        sent += [message for message, _ in messages]
        if stage == 0:
            for i in range(1, LEVELS):
                split_level(i)
            near_v[...] = jnp.zeros_like(near_v)
            tile_v[1] = jnp.zeros((TEAM, WIDTH, WIDTH), bf16)
        if stage == 2:
            halo_copies = halo_start()
        if SHARE[stage]:
            lax.fori_loop(done, done + SHARE[stage], near_step, 0)
            done += SHARE[stage]
            if done == STEPS:
                near_add(2 * STEPS - 1, 1)
        if stage == 3:
            halo_copies[0].wait_recv()
            halo_copies[1].wait_recv()
            edge_v[BOUND] = jnp.zeros((CLASSES, WIDTH), f32)
            near_edges()
            copies["res"].wait()
            curve, norm = finish_near()
            matrix, quad = coupled(0, None)
            for i in range(1, 5):
                matrix, more = coupled(i, matrix)
                quad = quad + 0.5**i * more
            lo_first = spread(as_row(curve + quad, norm), lo_out, lo_in, lo_s, lo_r, 0, lo_id, lo_peer)
        if stage == 4:
            matrix, quad = coupled(5, matrix)
            matrix, more = coupled(6, matrix)
            quad = 0.5 * quad + 0.25 * more
        given = []
        for message, at in messages:
            message.wait_recv()
            given.append((tree_in[at, :CLASSES], tree_in[at, CLASSES:]))
        node = plus(gift, given[0])
        level += 1
        keep(level, node)
        if len(masks) == 3:
            other = plus(given[1], given[2])
            half = halves[level]
            node = plus(raised(level, half, node), raised(level, 1 - half, other))
            level += 1
            keep(level, node)

    matrix, more = coupled(7, matrix)
    row = total(lo_first, lo_in, 0) + as_row(quad + 0.125 * more, jnp.zeros_like(quad))
    hi_first = spread(row, hi_out, hi_in, hi_s, hi_r, 0, hi_id, hi_peer)
    _, top = coupled(8, matrix)
    top = as_row(top, jnp.zeros_like(top))
    descent = lax.fori_loop(1, LEVELS + 1, lambda i, total: total + descent_v[i], descent_v[0])
    dh, dl = split2(descent)
    both = jnp.concatenate([dh, dl], axis=0)

    def image(k, carry):
        cols = pl.ds(pl.multiple_of(k * WIDTH, WIDTH), WIDTH)
        far = dot(both, basis_h[:, cols])
        far = far[:CLASSES] + far[CLASSES:] + dot(dh, basis_l[:, cols])
        near_v[k] = near_v[k] + far
        return carry

    lax.fori_loop(0, LEAVES, image, 0, unroll=2)
    row = total(hi_first, hi_in, 0) + top
    sums = as_columns(row)
    norm_old = sums[CLASSES:]
    step_size = norm_old / sums[:CLASSES]
    wide_step = jnp.concatenate([step_size, step_size], axis=1)

    def update(k, norm):
        cols = pl.ds(pl.multiple_of(k * WIDTH, WIDTH), WIDTH)
        new = res_v[:, cols] - wide_step * near_v[k]
        nr_ref[:, cols] = new
        return norm + lane_sums(new * new)

    norm = lax.fori_loop(0, LEAVES, update, jnp.zeros((CLASSES, RANK), f32))
    row = as_row(norm, jnp.zeros_like(norm))
    lo_second = spread(row, lo_out, lo_in, lo_s, lo_r, 1, lo_id, lo_peer)
    for message in sent + halo_copies:
        message.wait_send()
    for send, _ in lo_first + hi_first:
        send.wait_send()
    row = total(lo_second, lo_in, 1)
    hi_second = spread(row, hi_out, hi_in, hi_s, hi_r, 1, hi_id, hi_peer)
    for send, _ in lo_second:
        send.wait_send()
    row = total(hi_second, hi_in, 1)
    ab_ref[0] = step_size
    ab_ref[1] = as_columns(row)[:CLASSES] / norm_old

    for send, _ in hi_second:
        send.wait_send()


def finish(factors, sol_ref, nr_ref, dir_ref, new_sol_ref, new_res_ref, new_dir_ref):
    wide = lambda x: jnp.concatenate([x] * (FINISH // RANK), axis=1)
    d = dir_ref[...]
    nr = nr_ref[...]
    new_sol_ref[...] = sol_ref[...] + wide(factors[0]) * d
    new_res_ref[...] = nr
    new_dir_ref[...] = nr + wide(factors[1]) * d


def on_device(
    features, solution, residual, direction, neighbours,
    skeleton_basis, base_skeleton, upper_skeleton, transfer,
):
    classes, points = direction.shape
    vmem = pl.BlockSpec(memory_space=pltpu.VMEM)
    whole = pl.BlockSpec(memory_space=pl.ANY)
    dma = pltpu.SemaphoreType.DMA
    new_residual, factors = pl.pallas_call(
        kernel,
        out_shape=(
            jax.ShapeDtypeStruct((classes, points), f32),
            jax.ShapeDtypeStruct((2, classes, RANK), f32),
        ),
        in_specs=[whole, vmem, vmem, vmem, whole, whole, whole, whole],
        out_specs=(vmem, vmem),
        scratch_shapes=[
            pltpu.VMEM((classes, points), f32),
            pltpu.VMEM((classes, points), f32),
            pltpu.VMEM((RANK, points), f32),
            pltpu.VMEM((LEVELS, 2 * RANK, RANK), f32),
            pltpu.VMEM((RANK, points), bf16),
            pltpu.VMEM((RANK, points), bf16),
            pltpu.VMEM((LEVELS, 2 * RANK, RANK), bf16),
            pltpu.VMEM((LEVELS, 2 * RANK, RANK), bf16),
            pltpu.VMEM((LEVELS, 2 * RANK, RANK), bf16),
            pltpu.VMEM((LEAVES, WIDTH, 16), bf16),
            pltpu.VMEM((LEAVES, 16, WIDTH), bf16),
            pltpu.VMEM((LEAVES, CLASSES + 16, WIDTH), bf16),
            pltpu.VMEM((LEAVES, CLASSES, WIDTH), f32),
            pltpu.VMEM((9, CLASSES, WIDTH), f32),
            pltpu.VMEM((2, TEAM, WIDTH, WIDTH), bf16),
            pltpu.SMEM((8, LEAVES), jnp.int32),
            pltpu.SMEM((2, LEAVES), jnp.int32),
            pltpu.VMEM((LEVELS + 1, CLASSES + DIMS, RANK), f32),
            pltpu.VMEM((LEVELS + 1, CLASSES, RANK), f32),
            pltpu.VMEM((len(STAGES), CLASSES + DIMS, RANK), f32),
            pltpu.VMEM((MESSAGES, CLASSES + DIMS, RANK), f32),
            pltpu.VMEM((2, BOUND, CLASSES + 16, WIDTH), bf16),
            pltpu.VMEM((2, BOUND, CLASSES + 16, WIDTH), bf16),
            pltpu.VMEM((2, 1, RANK), f32),
            pltpu.VMEM((2, GROUP, 1, RANK), f32),
            pltpu.VMEM((2, 1, RANK), f32),
            pltpu.VMEM((2, GROUP, 1, RANK), f32),
            dma((8,)),
            dma((MESSAGES,)),
            dma((MESSAGES,)),
            dma((2,)),
            dma((2,)),
            dma((2, GROUP)),
            dma((2, GROUP)),
            dma((2, GROUP)),
            dma((2, GROUP)),
        ],
        compiler_params=pltpu.CompilerParams(
            collective_id=0, has_side_effects=True, vmem_limit_bytes=60 * 1024 * 1024
        ),
        name="cg_step",
    )(neighbours.T, base_skeleton, upper_skeleton, features, direction, residual, skeleton_basis, transfer)
    block = pl.BlockSpec((classes, FINISH), lambda i: (0, i))
    return pl.pallas_call(
        finish,
        grid=(points // FINISH,),
        out_shape=[jax.ShapeDtypeStruct((classes, points), f32)] * 3,
        in_specs=[pl.BlockSpec((2, classes, RANK), lambda i: (0, 0, 0)), block, block, block],
        out_specs=[block] * 3,
        name="cg_finish",
    )(factors, solution, new_residual, direction)


def solution(mesh):
    placed = (
        P(None, "leaf"),
        P(None, "leaf"),
        P(None, "leaf"),
        P(None, "leaf"),
        P("leaf", None),
        P(None, "leaf"),
        P("leaf", None),
        P("leaf", None, None),
        P("leaf", None, None, None),
    )
    return jax.shard_map(
        on_device,
        mesh=mesh,
        in_specs=placed,
        out_specs=(P(None, "leaf"), P(None, "leaf"), P(None, "leaf")),
        check_vma=False,
    )
```

```python
import functools

import jax
import jax.numpy as jnp
from jax import lax
from jax.experimental import pallas as pl
from jax.experimental.pallas import tpu as pltpu
from jax.sharding import PartitionSpec as P

f32 = jnp.float32
bf16 = jnp.bfloat16
MESH = pl.DeviceIdType.MESH
NN = (((1,), (0,)), ((), ()))
NT = (((1,), (1,)), ((), ()))

LEVELS = 8
GROUP = 16
LEAVES = 16
WIDTH = 256
INNER = 6
BOUND = 4
RANK = 128
CLASSES = 64
DIMS = 8
CHUNK = 512
FINISH = 2048
STAGES = ((1,), (2, 4, 6), (14,), (16, 32, 48), (64, 128, 192))
FAR_FIRST = (8, 7, 9, 6, 10, 5, 11, 4, 12, 3, 13, 2, 14, 1, 15)
MESSAGES = sum(len(stage) for stage in STAGES)
TEAM = 4
OWN_STEPS = LEAVES // TEAM // 2
PAIRS = LEAVES * INNER // 2
PAIR_STEPS = PAIRS // TEAM // 2
NOTHING = PAIRS
UPPER = 64
AFTER = UPPER + PAIRS
BEFORE = AFTER + BOUND
PLACES = BEFORE + BOUND
SHARE = (0, 2, 2, 2, 0)


def flip(me, mask):
    out = me
    for bit in range(LEVELS):
        if mask >> bit & 1:
            out = out + (1 - 2 * (me // 2**bit % 2)) * 2**bit
    return out


def dot(a, b, dims=NN):
    return lax.dot_general(a, b, dims, preferred_element_type=f32)


def split2(x):
    high = x.astype(bf16)
    return high, (x - high.astype(f32)).astype(bf16)


def split3(x):
    high = x.astype(bf16).astype(f32)
    rest = x - high
    mid = rest.astype(bf16).astype(f32)
    return high, mid, (rest - mid).astype(bf16).astype(f32)


def dot3(a, b, dims=NN):
    (ah, al), (bh, bl) = a, b
    rows = ah.shape[0]
    both = dot(jnp.concatenate([ah, al], axis=0), bh, dims)
    return both[:rows] + both[rows:] + dot(ah, bl, dims)


def norm_rows(norm, scale, swapped):
    high, mid, low = split3(norm)
    shape = (8, norm.shape[1])
    row = lax.broadcasted_iota(jnp.int32, shape, 0)
    first = 3 if swapped else 0
    ones = 0 if swapped else 3
    out = jnp.where((row >= ones) & (row < ones + 3), 1.0, 0.0).astype(f32)
    for i, piece in enumerate((high, mid, low)):
        out = jnp.where(row == first + i, jnp.broadcast_to(piece, shape), out)
    return out * scale


def gaussian(points):
    h, m, l = split3(points)
    norm = jnp.sum(points * points, axis=0, keepdims=True)
    pad = jnp.zeros_like(points)
    left = jnp.concatenate([h, h, m, h, m, l, norm_rows(norm, 1.0, False), pad], axis=0)
    right = jnp.concatenate(
        [0.25 * h, 0.25 * m, 0.25 * h, 0.25 * l, 0.25 * m, 0.25 * h, norm_rows(norm, -0.125, True), pad],
        axis=0,
    )
    return jnp.exp(dot(left.T.astype(bf16), right.astype(bf16)))


def pick(points, chosen):
    h, m, l = split3(points)
    stack = jnp.concatenate([h, m, l, jnp.zeros_like(h)], axis=0).astype(bf16)
    out = dot(stack, chosen)
    return (out[0:8] + out[8:16]) + out[16:24]


def one_hot(index_row, start, rows):
    at = lax.broadcasted_iota(jnp.int32, (rows, index_row.shape[1]), 0) + start
    return jnp.where(at == index_row, 1.0, 0.0).astype(bf16)


def kernel(
    nbr_any, base_any, upper_any, feat_any, dir_any, res_any, basis_any, trans_any,
    nr_any, ab_ref,
    nbr_v, base_ref, upper_ref, feat_ref, nr_v,
    dir_v, res_v, basis_v, trans_v, basis_h, basis_l, trans_h, trans_l, hots,
    source_v, target_v, value_v, near_v, product_v, tile_v, table_v, nbr, table_s, pos_s,
    node_v, descent_v, tree_out, tree_in, halo_out, halo_in, lo_out, lo_in, hi_out, hi_in,
    local_sem, tree_s, tree_r, halo_s, halo_r, lo_s, lo_r, hi_s, hi_r,
):
    me = lax.axis_index("leaf")
    lo_id = me % GROUP
    hi_id = me // GROUP
    halves = [me // 2**level % 2 for level in range(LEVELS)]

    barrier = pltpu.get_barrier_semaphore()
    right = (me + 1) % 256
    left = (me + 255) % 256
    peers = [right, left]
    peers += [hi_id * GROUP + (lo_id + m) % GROUP for m in range(1, GROUP)]
    peers += [(me + GROUP * m) % 256 for m in range(1, GROUP)]
    for peer in peers:
        pl.semaphore_signal(barrier, inc=1, device_id=(peer,), device_id_type=MESH)

    copies = {}
    copies["nbr"] = pltpu.make_async_copy(nbr_any, nbr, local_sem.at[7])
    copies["nbr"].start()
    quarter = basis_v.shape[1] // 4
    for at, (name, source, into) in enumerate((
        ("feat", feat_any, feat_ref), ("base", base_any, base_ref),
        ("upper", upper_any, upper_ref), ("nbr_v", nbr_any, nbr_v),
    )):
        copies[name] = pltpu.make_async_copy(source, into, local_sem.at[8 + at])
        copies[name].start()
    copies["dir"] = pltpu.make_async_copy(dir_any, dir_v, local_sem.at[0])
    copies["dir"].start()
    for i in range(4):
        cols = pl.ds(i * quarter, quarter)
        copies[i] = pltpu.make_async_copy(basis_any.at[:, cols], basis_v.at[:, cols], local_sem.at[1 + i])
        copies[i].start()
    copies["trans"] = pltpu.make_async_copy(trans_any.at[0], trans_v, local_sem.at[5])
    copies["trans"].start()
    copies["res"] = pltpu.make_async_copy(res_any, res_v, local_sem.at[6])
    copies["res"].start()

    copies["nbr"].wait()
    edges = []
    for slot in (6, 7):
        count = jnp.int32(0)
        mine = [jnp.int32(0)] * BOUND
        theirs = [jnp.int32(0)] * BOUND
        for k in range(LEAVES):
            partner = nbr[slot, k]
            filled = partner >= 0
            place = jnp.minimum(count, BOUND - 1) + (BEFORE if slot == 6 else AFTER)
            pos_s[slot - 6, k] = jnp.where(filled, place, NOTHING)
            for q in range(BOUND):
                here = filled & (count == q)
                mine[q] = jnp.where(here, k, mine[q])
                theirs[q] = jnp.where(here, partner, theirs[q])
            count = count + filled.astype(jnp.int32)
        ranks = []
        for q in range(BOUND):
            rank = jnp.int32(0)
            for p in range(BOUND):
                if p != q:
                    rank = rank + (theirs[p] < theirs[q]).astype(jnp.int32)
            ranks.append(jnp.minimum(rank, BOUND - 1))
        edges.append((mine, ranks))

    points = jnp.zeros((32, RANK), f32)
    copies["feat"].wait()
    copies["base"].wait()
    base_row = base_ref[...]
    for c in range(feat_ref.shape[1] // CHUNK):
        feat = feat_ref[:, c * CHUNK : (c + 1) * CHUNK]
        h, m, l = split3(feat)
        stack = jnp.concatenate([h, m, l, jnp.zeros_like(h)], axis=0).astype(bf16)
        points = points + dot(stack, one_hot(base_row, c * CHUNK, CHUNK))
        norm = jnp.sum(h * h, axis=0, keepdims=True)
        source = jnp.concatenate([h, norm_rows(norm, 1.0, False)], axis=0)
        target = jnp.concatenate([0.25 * h, norm_rows(norm, -0.125, True)], axis=0)
        for i in range(CHUNK // WIDTH):
            k = c * (CHUNK // WIDTH) + i
            block = source[:, i * WIDTH : (i + 1) * WIDTH]
            value_v[k, CLASSES:, :] = block.astype(bf16)
            source_v[k] = block.T.astype(bf16)
            target_v[k] = target[:, i * WIDTH : (i + 1) * WIDTH].astype(bf16)
    points = (points[0:8] + points[8:16]) + points[16:24]

    copies["dir"].wait()
    weights = jnp.zeros((CLASSES, RANK), f32)
    for c in range(dir_v.shape[1] // CHUNK):
        if c % (quarter // CHUNK) == 0:
            copies[c // (quarter // CHUNK)].wait()
        cols = slice(c * CHUNK, (c + 1) * CHUNK)
        dh, dl = split2(dir_v[:, cols])
        bh, bl = split2(basis_v[:, cols])
        basis_h[:, cols] = bh
        basis_l[:, cols] = bl
        for i in range(CHUNK // WIDTH):
            value_v[c * (CHUNK // WIDTH) + i, :CLASSES, :] = dh[:, i * WIDTH : (i + 1) * WIDTH]
        weights = weights + dot3((dh, dl), (bh, bl), NT)

    pl.semaphore_wait(barrier, len(peers))

    def tile(source, k):
        return jnp.exp(dot(source, target_v[k])).astype(bf16)

    def own_add(batch, buffer, *members):
        for member in members or range(TEAM):
            k = batch * TEAM + member
            near_v[k] = dot(value_v[k, :CLASSES, :], tile_v[buffer, member])

    def own_batch(batch, buffer):
        for member in range(TEAM):
            k = batch * TEAM + member
            tile_v[buffer, member] = tile(source_v[k], k)
        own_add(jnp.maximum(batch - 1, 0), 1 - buffer)

    def own_step(step, carry):
        own_batch(2 * step, 0)
        own_batch(2 * step + 1, 1)
        return carry

    def leaf_of(row, p):
        return jnp.clip(table_s[row, p], 0, LEAVES - 1)

    def pair_add(batch, buffer, *members):
        for member in members or range(TEAM):
            p = batch * TEAM + member
            block = tile_v[buffer, member]
            product_v[p] = dot(value_v[leaf_of(1, p), :CLASSES, :], block)
            product_v[UPPER + p] = dot(value_v[leaf_of(0, p), :CLASSES, :], block, NT)

    def pair_batch(batch, buffer):
        for member in range(TEAM):
            p = batch * TEAM + member
            tile_v[buffer, member] = tile(source_v[leaf_of(1, p)], leaf_of(0, p))
            pair_add(jnp.maximum(batch - 1, 0), 1 - buffer, member)

    def pair_step(step, carry):
        pair_batch(2 * step, 0)
        pair_batch(2 * step + 1, 1)
        return carry

    def list_pairs():
        square = (RANK, RANK)
        lane = lax.broadcasted_iota(jnp.int32, square, 1)
        sub = lax.broadcasted_iota(jnp.int32, square, 0)
        local = nbr_v[...] - me * LEAVES
        local = jnp.where((nbr_v[...] >= 0) & (local >= 0) & (local < LEAVES), local, -1)
        copies_of = jnp.where(lane[:LEAVES] % LEAVES == sub[:LEAVES], 1.0, 0.0).astype(bf16)
        spread_out = dot(local.astype(f32).astype(bf16), copies_of)
        mine = (lane[:8] // LEAVES == sub[:8]) & (sub[:8] < INNER)
        partner = jnp.sum(jnp.where(mine, spread_out, 0.0), axis=0, keepdims=True)
        partner = jnp.where(lane[:1] < INNER * LEAVES, partner, -1.0)
        partner_lane = jnp.broadcast_to(partner, square)
        partner_sub = partner_lane.T
        leaf_lane = (lane % LEAVES).astype(f32)
        leaf_sub = (sub % LEAVES).astype(f32)
        first_lane = partner_lane > leaf_lane
        first_sub = partner_sub > leaf_sub
        rank = jnp.sum(jnp.where(first_sub & (sub < lane), 1.0, 0.0), axis=0, keepdims=True)
        rank_sub = jnp.broadcast_to(rank, square).T
        here = first_sub & (rank_sub == lane.astype(f32))
        lower = jnp.sum(jnp.where(here, leaf_sub, 0.0), axis=0, keepdims=True)
        upper = jnp.sum(jnp.where(here, partner_sub, 0.0), axis=0, keepdims=True)
        met = first_sub & (leaf_sub == partner_lane) & (partner_sub == leaf_lane)
        back = jnp.max(jnp.where(met, rank_sub, 0.0), axis=0, keepdims=True)
        place = jnp.where(first_lane[:1], rank, jnp.where(partner >= 0.0, UPPER + back, float(NOTHING)))
        place = jnp.clip(place, 0.0, float(AFTER - 1))
        table_v[0:1] = lower.astype(jnp.int32)
        table_v[1:2] = upper.astype(jnp.int32)
        table_v[2:3] = place.astype(jnp.int32)
        move = pltpu.make_async_copy(table_v, table_s, local_sem.at[7])
        move.start()
        return move

    def near_edges():
        for side, at in ((1, AFTER), (0, BEFORE)):
            mine, ranks = edges[side]
            for q in range(BOUND):
                source = halo_in[side, ranks[q], CLASSES:].astype(f32).T.astype(bf16)
                tile_v[side, q] = tile(source, mine[q])
        for side, at in ((1, AFTER), (0, BEFORE)):
            ranks = edges[side][1]
            for q in range(BOUND):
                product_v[at + q] = dot(halo_in[side, ranks[q], :CLASSES], tile_v[side, q])

    def lane_sums(x):
        out = x[:, :RANK]
        for i in range(1, x.shape[1] // RANK):
            out = out + x[:, i * RANK : (i + 1) * RANK]
        return out

    def as_row(top, bottom):
        return jnp.sum(jnp.concatenate([top, bottom], axis=0).T, axis=0, keepdims=True)

    def as_columns(row):
        return jnp.broadcast_to(row, (RANK, RANK)).T

    def spread(row, out, into, sems, recvs, use, own_id, where):
        out[use] = row
        into[use, own_id] = row
        started = []
        for m in FAR_FIRST:
            peer, slot = where(m)
            send = pltpu.make_async_remote_copy(
                src_ref=out.at[use], dst_ref=into.at[use, own_id],
                send_sem=sems.at[use, m], recv_sem=recvs.at[use, own_id],
                device_id=(peer,), device_id_type=MESH,
            )
            send.start()
            arrival = pltpu.make_async_remote_copy(
                src_ref=out.at[use], dst_ref=into.at[use, slot],
                send_sem=sems.at[use, m], recv_sem=recvs.at[use, slot],
                device_id=(peer,), device_id_type=MESH,
            )
            started.append((send, arrival))
        return started

    def lo_peer(m):
        slot = (lo_id + m) % GROUP
        return hi_id * GROUP + slot, slot

    def hi_peer(m):
        slot = (hi_id + m) % GROUP
        return slot * GROUP + lo_id, slot

    def total(started, into, use):
        for _, arrival in started:
            arrival.wait_recv()
        return jnp.sum(into[use], axis=0)

    def halo_start():
        started = []
        for side, target in ((0, left), (1, right)):
            leaves = edges[side][0]
            for q in range(BOUND):
                halo_out[side, q] = value_v[leaves[q]]
            halo = pltpu.make_async_remote_copy(
                src_ref=halo_out.at[side], dst_ref=halo_in.at[1 - side],
                send_sem=halo_s.at[side], recv_sem=halo_r.at[1 - side],
                device_id=(target,), device_id_type=MESH,
            )
            halo.start()
            started.append(halo)
        return started

    def split_level(level):
        th, tl = split2(trans_v[level])
        trans_h[level] = th
        trans_l[level] = tl
        hots[level] = one_hot(upper_ref[0, level : level + 1, :], 0, 2 * RANK)

    def raised(level, half, node):
        rows = pl.ds(pl.multiple_of(half * RANK, RANK), RANK)
        step = (trans_h[level, rows], trans_l[level, rows])
        return (
            dot3(split2(node[0]), step),
            pick(node[1], hots[level, rows]),
        )

    def plus(a, b):
        return (a[0] + b[0], a[1] + b[1])

    def keep(level, node):
        node_v[level, :CLASSES] = node[0]
        node_v[level, CLASSES:] = node[1]

    def coupled(level, matrix):
        weights = node_v[level, :CLASSES]
        couple = dot3(split2(weights), split2(gaussian(node_v[level, CLASSES:])))
        if level == 0:
            descent_v[0] = couple
            return None, weights * couple
        half = halves[level - 1]
        rows = pl.ds(pl.multiple_of(half * RANK, RANK), RANK)
        if level == 1:
            matrix = trans_v[0, rows]
        else:
            matrix = dot3(split2(matrix), (trans_h[level - 1, rows], trans_l[level - 1, rows]))
        descent_v[level] = dot3(split2(couple), split2(matrix.T))
        return matrix, weights * couple

    def finish_near():
        def finish_leaf(k, carry):
            curve, norm = carry
            cols = pl.ds(pl.multiple_of(k * WIDTH, WIDTH), WIDTH)
            d = dir_v[:, cols]
            sides = product_v[pos_s[0, k]] + product_v[pos_s[1, k]]
            for s in range(INNER):
                sides = sides + product_v[jnp.clip(table_s[2, s * LEAVES + k], 0, AFTER - 1)]
            near = d + (near_v[k] + 0.125 * sides)
            near_v[k] = near
            r = res_v[:, cols]
            return curve + lane_sums(d * near), norm + lane_sums(r * r)

        zero = jnp.zeros((CLASSES, RANK), f32)
        return lax.fori_loop(0, LEAVES, finish_leaf, (zero, zero))

    sent = []
    level = 0
    slot = 0
    done = 0
    node = (weights, points)
    keep(0, node)
    copies["trans"].wait()
    copies["upper"].wait()
    split_level(0)
    for stage, masks in enumerate(STAGES):
        gift = raised(level, halves[level], node)
        tree_out[stage, :CLASSES] = gift[0]
        tree_out[stage, CLASSES:] = gift[1]
        messages = []
        for mask in masks:
            message = pltpu.make_async_remote_copy(
                src_ref=tree_out.at[stage], dst_ref=tree_in.at[slot],
                send_sem=tree_s.at[slot], recv_sem=tree_r.at[slot],
                device_id=(flip(me, mask),), device_id_type=MESH,
            )
            message.start()
            messages.append((message, slot))
            slot += 1
        sent += [message for message, _ in messages]
        if stage == 0:
            for i in range(1, LEVELS):
                split_level(i)
            copies["nbr_v"].wait()
            table_move = list_pairs()
            tile_v[1] = jnp.zeros((TEAM, WIDTH, WIDTH), bf16)
        if stage == 2:
            halo_copies = halo_start()
        if SHARE[stage]:
            if done == 0:
                matrix, quad = coupled(0, None)
                lax.fori_loop(0, OWN_STEPS, own_step, 0)
                own_add(2 * OWN_STEPS - 1, 1)
                table_move.wait()
            lax.fori_loop(done, done + SHARE[stage], pair_step, 0)
            done += SHARE[stage]
            for i in range(max(1, 2 * stage - 2), min(5, 2 * stage)):
                matrix, more = coupled(i, matrix)
                quad = quad + 0.5**i * more
            if done == PAIR_STEPS:
                pair_add(2 * PAIR_STEPS - 1, 1)
        if stage == 3:
            halo_copies[0].wait_recv()
            halo_copies[1].wait_recv()
            product_v[NOTHING] = jnp.zeros((CLASSES, WIDTH), f32)
            near_edges()
            copies["res"].wait()
            curve, norm = finish_near()
            lo_first = spread(as_row(curve + quad, norm), lo_out, lo_in, lo_s, lo_r, 0, lo_id, lo_peer)
        if stage == 4:
            matrix, quad = coupled(5, matrix)
            matrix, more = coupled(6, matrix)
            row = total(lo_first, lo_in, 0) + as_row(0.5 * quad + 0.25 * more, jnp.zeros_like(quad))
            hi_first = spread(row, hi_out, hi_in, hi_s, hi_r, 0, hi_id, hi_peer)
        given = []
        for message, at in messages:
            message.wait_recv()
            given.append((tree_in[at, :CLASSES], tree_in[at, CLASSES:]))
        node = plus(gift, given[0])
        level += 1
        keep(level, node)
        if len(masks) == 3:
            other = plus(given[1], given[2])
            half = halves[level]
            node = plus(raised(level, half, node), raised(level, 1 - half, other))
            level += 1
            keep(level, node)

    matrix, top = coupled(7, matrix)
    top = top + other[0] * dot3(split2(other[0]), split2(gaussian(other[1])))
    _, more = coupled(8, matrix)
    top = as_row(top + more, jnp.zeros_like(top))
    descent = lax.fori_loop(1, LEVELS + 1, lambda i, total: total + descent_v[i], descent_v[0])
    dh, dl = split2(descent)
    both = jnp.concatenate([dh, dl], axis=0)

    def image(k, carry):
        cols = pl.ds(pl.multiple_of(k * WIDTH, WIDTH), WIDTH)
        far = dot(both, basis_h[:, cols])
        far = far[:CLASSES] + far[CLASSES:] + dot(dh, basis_l[:, cols])
        near_v[k] = near_v[k] + far
        return carry

    lax.fori_loop(0, LEAVES, image, 0, unroll=2)
    row = total(hi_first, hi_in, 0) + top
    sums = as_columns(row)
    norm_old = sums[CLASSES:]
    step_size = norm_old / sums[:CLASSES]
    wide_step = jnp.concatenate([step_size, step_size], axis=1)

    def update(k, norm):
        cols = pl.ds(pl.multiple_of(k * WIDTH, WIDTH), WIDTH)
        new = res_v[:, cols] - wide_step * near_v[k]
        nr_v[:, cols] = new
        return norm + lane_sums(new * new)

    norm = lax.fori_loop(0, LEAVES, update, jnp.zeros((CLASSES, RANK), f32))
    row = as_row(norm, jnp.zeros_like(norm))
    lo_second = spread(row, lo_out, lo_in, lo_s, lo_r, 1, lo_id, lo_peer)
    nr_copy = pltpu.make_async_copy(nr_v, nr_any, local_sem.at[12])
    nr_copy.start()
    for message in sent + halo_copies:
        message.wait_send()
    for send, _ in lo_first + hi_first:
        send.wait_send()
    row = total(lo_second, lo_in, 1)
    hi_second = spread(row, hi_out, hi_in, hi_s, hi_r, 1, hi_id, hi_peer)
    for send, _ in lo_second:
        send.wait_send()
    row = total(hi_second, hi_in, 1)
    nr_copy.wait()
    ab_ref[0] = step_size
    ab_ref[1] = as_columns(row)[:CLASSES] / norm_old

    for send, _ in hi_second:
        send.wait_send()


def finish(factors, sol_ref, nr_ref, dir_ref, new_sol_ref, new_res_ref, new_dir_ref):
    wide = lambda x: jnp.concatenate([x] * (FINISH // RANK), axis=1)
    d = dir_ref[...]
    nr = nr_ref[...]
    new_sol_ref[...] = sol_ref[...] + wide(factors[0]) * d
    new_res_ref[...] = nr
    new_dir_ref[...] = nr + wide(factors[1]) * d


def on_device(
    features, solution, residual, direction, neighbours,
    skeleton_basis, base_skeleton, upper_skeleton, transfer,
):
    classes, points = direction.shape
    vmem = pl.BlockSpec(memory_space=pltpu.VMEM)
    whole = pl.BlockSpec(memory_space=pl.ANY)
    dma = pltpu.SemaphoreType.DMA
    new_residual, factors = pl.pallas_call(
        kernel,
        out_shape=(
            jax.ShapeDtypeStruct((classes, points), f32),
            jax.ShapeDtypeStruct((2, classes, RANK), f32),
        ),
        in_specs=[whole] * 8,
        out_specs=(whole, vmem),
        scratch_shapes=[
            pltpu.VMEM((8, LEAVES), jnp.int32),
            pltpu.VMEM((1, RANK), jnp.int32),
            pltpu.VMEM((1, LEVELS, RANK), jnp.int32),
            pltpu.VMEM((DIMS, points), f32),
            pltpu.VMEM((classes, points), f32),
            pltpu.VMEM((classes, points), f32),
            pltpu.VMEM((classes, points), f32),
            pltpu.VMEM((RANK, points), f32),
            pltpu.VMEM((LEVELS, 2 * RANK, RANK), f32),
            pltpu.VMEM((RANK, points), bf16),
            pltpu.VMEM((RANK, points), bf16),
            pltpu.VMEM((LEVELS, 2 * RANK, RANK), bf16),
            pltpu.VMEM((LEVELS, 2 * RANK, RANK), bf16),
            pltpu.VMEM((LEVELS, 2 * RANK, RANK), bf16),
            pltpu.VMEM((LEAVES, WIDTH, 16), bf16),
            pltpu.VMEM((LEAVES, 16, WIDTH), bf16),
            pltpu.VMEM((LEAVES, CLASSES + 16, WIDTH), bf16),
            pltpu.VMEM((LEAVES, CLASSES, WIDTH), f32),
            pltpu.VMEM((PLACES, CLASSES, WIDTH), f32),
            pltpu.VMEM((2, TEAM, WIDTH, WIDTH), bf16),
            pltpu.VMEM((8, RANK), jnp.int32),
            pltpu.SMEM((8, LEAVES), jnp.int32),
            pltpu.SMEM((8, RANK), jnp.int32),
            pltpu.SMEM((2, LEAVES), jnp.int32),
            pltpu.VMEM((LEVELS + 1, CLASSES + DIMS, RANK), f32),
            pltpu.VMEM((LEVELS + 1, CLASSES, RANK), f32),
            pltpu.VMEM((len(STAGES), CLASSES + DIMS, RANK), f32),
            pltpu.VMEM((MESSAGES, CLASSES + DIMS, RANK), f32),
            pltpu.VMEM((2, BOUND, CLASSES + 16, WIDTH), bf16),
            pltpu.VMEM((2, BOUND, CLASSES + 16, WIDTH), bf16),
            pltpu.VMEM((2, 1, RANK), f32),
            pltpu.VMEM((2, GROUP, 1, RANK), f32),
            pltpu.VMEM((2, 1, RANK), f32),
            pltpu.VMEM((2, GROUP, 1, RANK), f32),
            dma((13,)),
            dma((MESSAGES,)),
            dma((MESSAGES,)),
            dma((2,)),
            dma((2,)),
            dma((2, GROUP)),
            dma((2, GROUP)),
            dma((2, GROUP)),
            dma((2, GROUP)),
        ],
        compiler_params=pltpu.CompilerParams(
            collective_id=0, has_side_effects=True, vmem_limit_bytes=60 * 1024 * 1024
        ),
        name="cg_step",
    )(neighbours.T, base_skeleton, upper_skeleton, features, direction, residual, skeleton_basis, transfer)
    block = pl.BlockSpec((classes, FINISH), lambda i: (0, i))
    return pl.pallas_call(
        finish,
        grid=(points // FINISH,),
        out_shape=[jax.ShapeDtypeStruct((classes, points), f32)] * 3,
        in_specs=[pl.BlockSpec((2, classes, RANK), lambda i: (0, 0, 0)), block, block, block],
        out_specs=[block] * 3,
        name="cg_finish",
    )(factors, solution, new_residual, direction)


def solution(mesh):
    placed = (
        P(None, "leaf"),
        P(None, "leaf"),
        P(None, "leaf"),
        P(None, "leaf"),
        P("leaf", None),
        P(None, "leaf"),
        P("leaf", None),
        P("leaf", None, None),
        P("leaf", None, None, None),
    )
    return jax.shard_map(
        on_device,
        mesh=mesh,
        in_specs=placed,
        out_specs=(P(None, "leaf"), P(None, "leaf"), P(None, "leaf")),
        check_vma=False,
    )
```

```python
import functools

import jax
import jax.numpy as jnp
from jax import lax
from jax.experimental import pallas as pl
from jax.experimental.pallas import tpu as pltpu
from jax.sharding import PartitionSpec as P

f32 = jnp.float32
bf16 = jnp.bfloat16
MESH = pl.DeviceIdType.MESH
NN = (((1,), (0,)), ((), ()))
NT = (((1,), (1,)), ((), ()))

LEVELS = 8
GROUP = 16
LEAVES = 16
WIDTH = 256
INNER = 6
BOUND = 4
RANK = 128
CLASSES = 64
DIMS = 8
CHUNK = 512
FINISH = 2048
STAGES = ((1,), (2, 4, 6), (14,), (16, 32, 48), (64, 128, 192))
FAR_FIRST = (8, 7, 9, 6, 10, 5, 11, 4, 12, 3, 13, 2, 14, 1, 15)
MESSAGES = sum(len(stage) for stage in STAGES)
TEAM = 4
OWN_STEPS = LEAVES // TEAM // 2
PAIRS = LEAVES * INNER // 2
PAIR_STEPS = PAIRS // TEAM // 2
NOTHING = PAIRS
UPPER = 64
AFTER = UPPER + PAIRS
BEFORE = AFTER + BOUND
PLACES = BEFORE + BOUND
SHARE = (0, 2, 2, 2, 0)


def flip(me, mask):
    out = me
    for bit in range(LEVELS):
        if mask >> bit & 1:
            out = out + (1 - 2 * (me // 2**bit % 2)) * 2**bit
    return out


def dot(a, b, dims=NN):
    return lax.dot_general(a, b, dims, preferred_element_type=f32)


def split2(x):
    high = x.astype(bf16)
    return high, (x - high.astype(f32)).astype(bf16)


def split3(x):
    high = x.astype(bf16).astype(f32)
    rest = x - high
    mid = rest.astype(bf16).astype(f32)
    return high, mid, (rest - mid).astype(bf16).astype(f32)


def dot3(a, b, dims=NN):
    (ah, al), (bh, bl) = a, b
    rows = ah.shape[0]
    both = dot(jnp.concatenate([ah, al], axis=0), bh, dims)
    return both[:rows] + both[rows:] + dot(ah, bl, dims)


def norm_rows(norm, scale, swapped):
    high, mid, low = split3(norm)
    shape = (8, norm.shape[1])
    row = lax.broadcasted_iota(jnp.int32, shape, 0)
    first = 3 if swapped else 0
    ones = 0 if swapped else 3
    out = jnp.where((row >= ones) & (row < ones + 3), 1.0, 0.0).astype(f32)
    for i, piece in enumerate((high, mid, low)):
        out = jnp.where(row == first + i, jnp.broadcast_to(piece, shape), out)
    return out * scale


def gaussian(points):
    h, m, l = split3(points)
    norm = jnp.sum(points * points, axis=0, keepdims=True)
    pad = jnp.zeros_like(points)
    left = jnp.concatenate([h, h, m, h, m, l, norm_rows(norm, 1.0, False), pad], axis=0)
    right = jnp.concatenate(
        [0.25 * h, 0.25 * m, 0.25 * h, 0.25 * l, 0.25 * m, 0.25 * h, norm_rows(norm, -0.125, True), pad],
        axis=0,
    )
    return jnp.exp(dot(left.T.astype(bf16), right.astype(bf16)))


def pick(points, chosen):
    h, m, l = split3(points)
    stack = jnp.concatenate([h, m, l, jnp.zeros_like(h)], axis=0).astype(bf16)
    out = dot(stack, chosen)
    return (out[0:8] + out[8:16]) + out[16:24]


def one_hot(index_row, start, rows):
    at = lax.broadcasted_iota(jnp.int32, (rows, index_row.shape[1]), 0) + start
    return jnp.where(at == index_row, 1.0, 0.0).astype(bf16)


def kernel(
    nbr_any, base_any, upper_any, feat_any, dir_any, res_any, basis_any, trans_any,
    nr_any, ab_ref,
    nbr_v, base_ref, upper_ref, feat_ref, nr_v,
    dir_v, res_v, basis_v, trans_v, basis_h, basis_l, trans_h, trans_l, hots,
    source_v, target_v, value_v, near_v, product_v, tile_v, table_v, nbr, table_s, pos_s,
    node_v, descent_v, tree_out, tree_in, halo_out, halo_in, lo_out, lo_in, hi_out, hi_in,
    local_sem, tree_s, tree_r, halo_s, halo_r, lo_s, lo_r, hi_s, hi_r,
):
    me = lax.axis_index("leaf")
    lo_id = me % GROUP
    hi_id = me // GROUP
    halves = [me // 2**level % 2 for level in range(LEVELS)]

    barrier = pltpu.get_barrier_semaphore()
    right = (me + 1) % 256
    left = (me + 255) % 256
    peers = [right, left]
    peers += [hi_id * GROUP + (lo_id + m) % GROUP for m in range(1, GROUP)]
    peers += [(me + GROUP * m) % 256 for m in range(1, GROUP)]
    for peer in peers:
        pl.semaphore_signal(barrier, inc=1, device_id=(peer,), device_id_type=MESH)

    copies = {}
    copies["nbr"] = pltpu.make_async_copy(nbr_any, nbr, local_sem.at[7])
    copies["nbr"].start()
    quarter = basis_v.shape[1] // 4
    for at, (name, source, into) in enumerate((
        ("feat", feat_any, feat_ref), ("base", base_any, base_ref),
        ("upper", upper_any, upper_ref), ("nbr_v", nbr_any, nbr_v),
    )):
        copies[name] = pltpu.make_async_copy(source, into, local_sem.at[8 + at])
        copies[name].start()
    copies["dir"] = pltpu.make_async_copy(dir_any, dir_v, local_sem.at[0])
    copies["dir"].start()
    for i in range(4):
        cols = pl.ds(i * quarter, quarter)
        copies[i] = pltpu.make_async_copy(basis_any.at[:, cols], basis_v.at[:, cols], local_sem.at[1 + i])
        copies[i].start()
    copies["trans"] = pltpu.make_async_copy(trans_any.at[0], trans_v, local_sem.at[5])
    copies["trans"].start()
    copies["res"] = pltpu.make_async_copy(res_any, res_v, local_sem.at[6])
    copies["res"].start()

    copies["nbr"].wait()
    edges = []
    for slot in (6, 7):
        count = jnp.int32(0)
        mine = [jnp.int32(0)] * BOUND
        theirs = [jnp.int32(0)] * BOUND
        for k in range(LEAVES):
            partner = nbr[slot, k]
            filled = partner >= 0
            place = jnp.minimum(count, BOUND - 1) + (BEFORE if slot == 6 else AFTER)
            pos_s[slot - 6, k] = jnp.where(filled, place, NOTHING)
            for q in range(BOUND):
                here = filled & (count == q)
                mine[q] = jnp.where(here, k, mine[q])
                theirs[q] = jnp.where(here, partner, theirs[q])
            count = count + filled.astype(jnp.int32)
        ranks = []
        for q in range(BOUND):
            rank = jnp.int32(0)
            for p in range(BOUND):
                if p != q:
                    rank = rank + (theirs[p] < theirs[q]).astype(jnp.int32)
            ranks.append(jnp.minimum(rank, BOUND - 1))
        edges.append((mine, ranks))

    points = jnp.zeros((32, RANK), f32)
    copies["feat"].wait()
    copies["base"].wait()
    base_row = base_ref[...]
    for c in range(feat_ref.shape[1] // CHUNK):
        feat = feat_ref[:, c * CHUNK : (c + 1) * CHUNK]
        h, m, l = split3(feat)
        stack = jnp.concatenate([h, m, l, jnp.zeros_like(h)], axis=0).astype(bf16)
        points = points + dot(stack, one_hot(base_row, c * CHUNK, CHUNK))
        norm = jnp.sum(h * h, axis=0, keepdims=True)
        source = jnp.concatenate([h, norm_rows(norm, 1.0, False)], axis=0)
        target = jnp.concatenate([0.25 * h, norm_rows(norm, -0.125, True)], axis=0)
        for i in range(CHUNK // WIDTH):
            k = c * (CHUNK // WIDTH) + i
            block = source[:, i * WIDTH : (i + 1) * WIDTH]
            value_v[k, CLASSES:, :] = block.astype(bf16)
            source_v[k] = block.T.astype(bf16)
            target_v[k] = target[:, i * WIDTH : (i + 1) * WIDTH].astype(bf16)
    points = (points[0:8] + points[8:16]) + points[16:24]

    copies["dir"].wait()
    weights = jnp.zeros((CLASSES, RANK), f32)
    for c in range(dir_v.shape[1] // CHUNK):
        if c % (quarter // CHUNK) == 0:
            copies[c // (quarter // CHUNK)].wait()
        cols = slice(c * CHUNK, (c + 1) * CHUNK)
        dh, dl = split2(dir_v[:, cols])
        bh, bl = split2(basis_v[:, cols])
        basis_h[:, cols] = bh
        basis_l[:, cols] = bl
        for i in range(CHUNK // WIDTH):
            value_v[c * (CHUNK // WIDTH) + i, :CLASSES, :] = dh[:, i * WIDTH : (i + 1) * WIDTH]
        weights = weights + dot3((dh, dl), (bh, bl), NT)

    pl.semaphore_wait(barrier, len(peers))

    def tile(source, k):
        return jnp.exp(dot(source, target_v[k])).astype(bf16)

    def own_add(batch, buffer, *members):
        for member in members or range(TEAM):
            k = batch * TEAM + member
            near_v[k] = dot(value_v[k, :CLASSES, :], tile_v[buffer, member])

    def own_batch(batch, buffer):
        for member in range(TEAM):
            k = batch * TEAM + member
            tile_v[buffer, member] = tile(source_v[k], k)
        own_add(jnp.maximum(batch - 1, 0), 1 - buffer)

    def own_step(step, carry):
        own_batch(2 * step, 0)
        own_batch(2 * step + 1, 1)
        return carry

    def leaf_of(row, p):
        return jnp.clip(table_s[row, p], 0, LEAVES - 1)

    def pair_add(batch, buffer, *members):
        for member in members or range(TEAM):
            p = batch * TEAM + member
            block = tile_v[buffer, member]
            product_v[p] = dot(value_v[leaf_of(1, p), :CLASSES, :], block)
            product_v[UPPER + p] = dot(value_v[leaf_of(0, p), :CLASSES, :], block, NT)

    def pair_batch(batch, buffer):
        for member in range(TEAM):
            p = batch * TEAM + member
            tile_v[buffer, member] = tile(source_v[leaf_of(1, p)], leaf_of(0, p))
            pair_add(jnp.maximum(batch - 1, 0), 1 - buffer, member)

    def pair_step(step, carry):
        pair_batch(2 * step, 0)
        pair_batch(2 * step + 1, 1)
        return carry

    def list_pairs():
        square = (RANK, RANK)
        lane = lax.broadcasted_iota(jnp.int32, square, 1)
        sub = lax.broadcasted_iota(jnp.int32, square, 0)
        local = nbr_v[...] - me * LEAVES
        local = jnp.where((nbr_v[...] >= 0) & (local >= 0) & (local < LEAVES), local, -1)
        copies_of = jnp.where(lane[:LEAVES] % LEAVES == sub[:LEAVES], 1.0, 0.0).astype(bf16)
        spread_out = dot(local.astype(f32).astype(bf16), copies_of)
        mine = (lane[:8] // LEAVES == sub[:8]) & (sub[:8] < INNER)
        partner = jnp.sum(jnp.where(mine, spread_out, 0.0), axis=0, keepdims=True)
        partner = jnp.where(lane[:1] < INNER * LEAVES, partner, -1.0)
        partner_lane = jnp.broadcast_to(partner, square)
        partner_sub = partner_lane.T
        leaf_lane = (lane % LEAVES).astype(f32)
        leaf_sub = (sub % LEAVES).astype(f32)
        first_lane = partner_lane > leaf_lane
        first_sub = partner_sub > leaf_sub
        rank = jnp.sum(jnp.where(first_sub & (sub < lane), 1.0, 0.0), axis=0, keepdims=True)
        rank_sub = jnp.broadcast_to(rank, square).T
        here = first_sub & (rank_sub == lane.astype(f32))
        lower = jnp.sum(jnp.where(here, leaf_sub, 0.0), axis=0, keepdims=True)
        upper = jnp.sum(jnp.where(here, partner_sub, 0.0), axis=0, keepdims=True)
        met = first_sub & (leaf_sub == partner_lane) & (partner_sub == leaf_lane)
        back = jnp.max(jnp.where(met, rank_sub, 0.0), axis=0, keepdims=True)
        place = jnp.where(first_lane[:1], rank, jnp.where(partner >= 0.0, UPPER + back, float(NOTHING)))
        place = jnp.clip(place, 0.0, float(AFTER - 1))
        table_v[0:1] = lower.astype(jnp.int32)
        table_v[1:2] = upper.astype(jnp.int32)
        table_v[2:3] = place.astype(jnp.int32)
        move = pltpu.make_async_copy(table_v, table_s, local_sem.at[7])
        move.start()
        return move

    def near_edges():
        for side, at in ((1, AFTER), (0, BEFORE)):
            mine, ranks = edges[side]
            for q in range(BOUND):
                source = halo_in[side, ranks[q], CLASSES:].astype(f32).T.astype(bf16)
                tile_v[side, q] = tile(source, mine[q])
        for side, at in ((1, AFTER), (0, BEFORE)):
            ranks = edges[side][1]
            for q in range(BOUND):
                product_v[at + q] = dot(halo_in[side, ranks[q], :CLASSES], tile_v[side, q])

    def lane_sums(x):
        out = x[:, :RANK]
        for i in range(1, x.shape[1] // RANK):
            out = out + x[:, i * RANK : (i + 1) * RANK]
        return out

    def as_row(top, bottom):
        return jnp.sum(jnp.concatenate([top, bottom], axis=0).T, axis=0, keepdims=True)

    def as_columns(row):
        return jnp.broadcast_to(row, (RANK, RANK)).T

    def spread(row, out, into, sems, recvs, use, own_id, where):
        out[use] = row
        into[use, own_id] = row
        started = []
        for m in FAR_FIRST:
            peer, slot = where(m)
            send = pltpu.make_async_remote_copy(
                src_ref=out.at[use], dst_ref=into.at[use, own_id],
                send_sem=sems.at[use, m], recv_sem=recvs.at[use, own_id],
                device_id=(peer,), device_id_type=MESH,
            )
            send.start()
            arrival = pltpu.make_async_remote_copy(
                src_ref=out.at[use], dst_ref=into.at[use, slot],
                send_sem=sems.at[use, m], recv_sem=recvs.at[use, slot],
                device_id=(peer,), device_id_type=MESH,
            )
            started.append((send, arrival))
        return started

    def lo_peer(m):
        slot = (lo_id + m) % GROUP
        return hi_id * GROUP + slot, slot

    def hi_peer(m):
        slot = (hi_id + m) % GROUP
        return slot * GROUP + lo_id, slot

    def total(started, into, use):
        for _, arrival in started:
            arrival.wait_recv()
        return jnp.sum(into[use], axis=0)

    def halo_start():
        started = []
        for side, target in ((0, left), (1, right)):
            leaves = edges[side][0]
            for q in range(BOUND):
                halo_out[side, q] = value_v[leaves[q]]
            halo = pltpu.make_async_remote_copy(
                src_ref=halo_out.at[side], dst_ref=halo_in.at[1 - side],
                send_sem=halo_s.at[side], recv_sem=halo_r.at[1 - side],
                device_id=(target,), device_id_type=MESH,
            )
            halo.start()
            started.append(halo)
        return started

    def split_level(level):
        th, tl = split2(trans_v[level])
        trans_h[level] = th
        trans_l[level] = tl
        hots[level] = one_hot(upper_ref[0, level : level + 1, :], 0, 2 * RANK)

    def raised(level, half, node):
        rows = pl.ds(pl.multiple_of(half * RANK, RANK), RANK)
        step = (trans_h[level, rows], trans_l[level, rows])
        return (
            dot3(split2(node[0]), step),
            pick(node[1], hots[level, rows]),
        )

    def plus(a, b):
        return (a[0] + b[0], a[1] + b[1])

    def keep(level, node):
        node_v[level, :CLASSES] = node[0]
        node_v[level, CLASSES:] = node[1]

    def coupled(level, matrix):
        weights = node_v[level, :CLASSES]
        couple = dot3(split2(weights), split2(gaussian(node_v[level, CLASSES:])))
        if level == 0:
            descent_v[0] = couple
            return None, weights * couple
        half = halves[level - 1]
        rows = pl.ds(pl.multiple_of(half * RANK, RANK), RANK)
        if level == 1:
            matrix = trans_v[0, rows]
        else:
            matrix = dot3(split2(matrix), (trans_h[level - 1, rows], trans_l[level - 1, rows]))
        descent_v[level] = dot3(split2(couple), split2(matrix.T))
        return matrix, weights * couple

    def finish_near():
        def finish_leaf(k, carry):
            curve, norm = carry
            cols = pl.ds(pl.multiple_of(k * WIDTH, WIDTH), WIDTH)
            d = dir_v[:, cols]
            sides = product_v[pos_s[0, k]] + product_v[pos_s[1, k]]
            for s in range(INNER):
                sides = sides + product_v[jnp.clip(table_s[2, s * LEAVES + k], 0, AFTER - 1)]
            near = d + (near_v[k] + 0.125 * sides)
            near_v[k] = near
            r = res_v[:, cols]
            return curve + lane_sums(d * near), norm + lane_sums(r * r)

        zero = jnp.zeros((CLASSES, RANK), f32)
        return lax.fori_loop(0, LEAVES, finish_leaf, (zero, zero))

    sent = []
    level = 0
    slot = 0
    done = 0
    node = (weights, points)
    keep(0, node)
    copies["trans"].wait()
    copies["upper"].wait()
    split_level(0)
    for stage, masks in enumerate(STAGES):
        gift = raised(level, halves[level], node)
        tree_out[stage, :CLASSES] = gift[0]
        tree_out[stage, CLASSES:] = gift[1]
        messages = []
        for mask in masks:
            message = pltpu.make_async_remote_copy(
                src_ref=tree_out.at[stage], dst_ref=tree_in.at[slot],
                send_sem=tree_s.at[slot], recv_sem=tree_r.at[slot],
                device_id=(flip(me, mask),), device_id_type=MESH,
            )
            message.start()
            messages.append((message, slot))
            slot += 1
        sent += [message for message, _ in messages]
        if stage == 0:
            for i in range(1, LEVELS):
                split_level(i)
            copies["nbr_v"].wait()
            table_move = list_pairs()
            tile_v[1] = jnp.zeros((TEAM, WIDTH, WIDTH), bf16)
        if stage == 1:
            halo_copies = halo_start()
        if SHARE[stage]:
            if done == 0:
                matrix, quad = coupled(0, None)
                lax.fori_loop(0, OWN_STEPS, own_step, 0)
                own_add(2 * OWN_STEPS - 1, 1)
                table_move.wait()
            lax.fori_loop(done, done + SHARE[stage], pair_step, 0)
            done += SHARE[stage]
            for i in range(max(1, 2 * stage - 2), min(5, 2 * stage)):
                matrix, more = coupled(i, matrix)
                quad = quad + 0.5**i * more
            if done == PAIR_STEPS:
                pair_add(2 * PAIR_STEPS - 1, 1)
        if stage == 3:
            halo_copies[0].wait_recv()
            halo_copies[1].wait_recv()
            product_v[NOTHING] = jnp.zeros((CLASSES, WIDTH), f32)
            near_edges()
            copies["res"].wait()
            curve, norm = finish_near()
            lo_first = spread(as_row(curve + quad, norm), lo_out, lo_in, lo_s, lo_r, 0, lo_id, lo_peer)
        if stage == 4:
            matrix, quad = coupled(5, matrix)
            matrix, more = coupled(6, matrix)
            row = total(lo_first, lo_in, 0) + as_row(0.5 * quad + 0.25 * more, jnp.zeros_like(quad))
            hi_first = spread(row, hi_out, hi_in, hi_s, hi_r, 0, hi_id, hi_peer)
        given = []
        for message, at in messages:
            message.wait_recv()
            given.append((tree_in[at, :CLASSES], tree_in[at, CLASSES:]))
        node = plus(gift, given[0])
        level += 1
        keep(level, node)
        if len(masks) == 3:
            other = plus(given[1], given[2])
            half = halves[level]
            node = plus(raised(level, half, node), raised(level, 1 - half, other))
            level += 1
            keep(level, node)

    matrix, top = coupled(7, matrix)
    top = top + other[0] * dot3(split2(other[0]), split2(gaussian(other[1])))
    _, more = coupled(8, matrix)
    top = as_row(top + more, jnp.zeros_like(top))
    descent = lax.fori_loop(1, LEVELS + 1, lambda i, total: total + descent_v[i], descent_v[0])
    dh, dl = split2(descent)
    both = jnp.concatenate([dh, dl], axis=0)

    def image(k, carry):
        cols = pl.ds(pl.multiple_of(k * WIDTH, WIDTH), WIDTH)
        far = dot(both, basis_h[:, cols])
        far = far[:CLASSES] + far[CLASSES:] + dot(dh, basis_l[:, cols])
        near_v[k] = near_v[k] + far
        return carry

    lax.fori_loop(0, LEAVES, image, 0, unroll=2)
    row = total(hi_first, hi_in, 0) + top
    sums = as_columns(row)
    norm_old = sums[CLASSES:]
    step_size = norm_old / sums[:CLASSES]
    wide_step = jnp.concatenate([step_size, step_size], axis=1)

    def update(k, norm):
        cols = pl.ds(pl.multiple_of(k * WIDTH, WIDTH), WIDTH)
        new = res_v[:, cols] - wide_step * near_v[k]
        nr_v[:, cols] = new
        return norm + lane_sums(new * new)

    norm = lax.fori_loop(0, LEAVES, update, jnp.zeros((CLASSES, RANK), f32))
    row = as_row(norm, jnp.zeros_like(norm))
    lo_second = spread(row, lo_out, lo_in, lo_s, lo_r, 1, lo_id, lo_peer)
    nr_copy = pltpu.make_async_copy(nr_v, nr_any, local_sem.at[12])
    nr_copy.start()
    for message in sent + halo_copies:
        message.wait_send()
    for send, _ in lo_first + hi_first:
        send.wait_send()
    row = total(lo_second, lo_in, 1)
    hi_second = spread(row, hi_out, hi_in, hi_s, hi_r, 1, hi_id, hi_peer)
    for send, _ in lo_second:
        send.wait_send()
    row = total(hi_second, hi_in, 1)
    nr_copy.wait()
    ab_ref[0] = step_size
    ab_ref[1] = as_columns(row)[:CLASSES] / norm_old

    for send, _ in hi_second:
        send.wait_send()


def finish(factors, sol_ref, nr_ref, dir_ref, new_sol_ref, new_res_ref, new_dir_ref):
    wide = lambda x: jnp.concatenate([x] * (FINISH // RANK), axis=1)
    d = dir_ref[...]
    nr = nr_ref[...]
    new_sol_ref[...] = sol_ref[...] + wide(factors[0]) * d
    new_res_ref[...] = nr
    new_dir_ref[...] = nr + wide(factors[1]) * d


def on_device(
    features, solution, residual, direction, neighbours,
    skeleton_basis, base_skeleton, upper_skeleton, transfer,
):
    classes, points = direction.shape
    vmem = pl.BlockSpec(memory_space=pltpu.VMEM)
    whole = pl.BlockSpec(memory_space=pl.ANY)
    dma = pltpu.SemaphoreType.DMA
    new_residual, factors = pl.pallas_call(
        kernel,
        out_shape=(
            jax.ShapeDtypeStruct((classes, points), f32),
            jax.ShapeDtypeStruct((2, classes, RANK), f32),
        ),
        in_specs=[whole] * 8,
        out_specs=(whole, vmem),
        scratch_shapes=[
            pltpu.VMEM((8, LEAVES), jnp.int32),
            pltpu.VMEM((1, RANK), jnp.int32),
            pltpu.VMEM((1, LEVELS, RANK), jnp.int32),
            pltpu.VMEM((DIMS, points), f32),
            pltpu.VMEM((classes, points), f32),
            pltpu.VMEM((classes, points), f32),
            pltpu.VMEM((classes, points), f32),
            pltpu.VMEM((RANK, points), f32),
            pltpu.VMEM((LEVELS, 2 * RANK, RANK), f32),
            pltpu.VMEM((RANK, points), bf16),
            pltpu.VMEM((RANK, points), bf16),
            pltpu.VMEM((LEVELS, 2 * RANK, RANK), bf16),
            pltpu.VMEM((LEVELS, 2 * RANK, RANK), bf16),
            pltpu.VMEM((LEVELS, 2 * RANK, RANK), bf16),
            pltpu.VMEM((LEAVES, WIDTH, 16), bf16),
            pltpu.VMEM((LEAVES, 16, WIDTH), bf16),
            pltpu.VMEM((LEAVES, CLASSES + 16, WIDTH), bf16),
            pltpu.VMEM((LEAVES, CLASSES, WIDTH), f32),
            pltpu.VMEM((PLACES, CLASSES, WIDTH), f32),
            pltpu.VMEM((2, TEAM, WIDTH, WIDTH), bf16),
            pltpu.VMEM((8, RANK), jnp.int32),
            pltpu.SMEM((8, LEAVES), jnp.int32),
            pltpu.SMEM((8, RANK), jnp.int32),
            pltpu.SMEM((2, LEAVES), jnp.int32),
            pltpu.VMEM((LEVELS + 1, CLASSES + DIMS, RANK), f32),
            pltpu.VMEM((LEVELS + 1, CLASSES, RANK), f32),
            pltpu.VMEM((len(STAGES), CLASSES + DIMS, RANK), f32),
            pltpu.VMEM((MESSAGES, CLASSES + DIMS, RANK), f32),
            pltpu.VMEM((2, BOUND, CLASSES + 16, WIDTH), bf16),
            pltpu.VMEM((2, BOUND, CLASSES + 16, WIDTH), bf16),
            pltpu.VMEM((2, 1, RANK), f32),
            pltpu.VMEM((2, GROUP, 1, RANK), f32),
            pltpu.VMEM((2, 1, RANK), f32),
            pltpu.VMEM((2, GROUP, 1, RANK), f32),
            dma((13,)),
            dma((MESSAGES,)),
            dma((MESSAGES,)),
            dma((2,)),
            dma((2,)),
            dma((2, GROUP)),
            dma((2, GROUP)),
            dma((2, GROUP)),
            dma((2, GROUP)),
        ],
        compiler_params=pltpu.CompilerParams(
            collective_id=0, has_side_effects=True, vmem_limit_bytes=60 * 1024 * 1024
        ),
        name="cg_step",
    )(neighbours.T, base_skeleton, upper_skeleton, features, direction, residual, skeleton_basis, transfer)
    block = pl.BlockSpec((classes, FINISH), lambda i: (0, i))
    return pl.pallas_call(
        finish,
        grid=(points // FINISH,),
        out_shape=[jax.ShapeDtypeStruct((classes, points), f32)] * 3,
        in_specs=[pl.BlockSpec((2, classes, RANK), lambda i: (0, 0, 0)), block, block, block],
        out_specs=[block] * 3,
        name="cg_finish",
    )(factors, solution, new_residual, direction)


def solution(mesh):
    placed = (
        P(None, "leaf"),
        P(None, "leaf"),
        P(None, "leaf"),
        P(None, "leaf"),
        P("leaf", None),
        P(None, "leaf"),
        P("leaf", None),
        P("leaf", None, None),
        P("leaf", None, None, None),
    )
    return jax.shard_map(
        on_device,
        mesh=mesh,
        in_specs=placed,
        out_specs=(P(None, "leaf"), P(None, "leaf"), P(None, "leaf")),
        check_vma=False,
    )
```
